32 devices in a mesh: ctx: 8 (over y, x, core), mp: 4 (over z).
Axes of the slice: x: 2, y: 2, z: 4, core: 2. Of those that a mesh axis runs over, the one named last changes fastest.
Arguments:
- hyena_in: bfloat16 [3, 2048, 1024], P(None, 'ctx', 'mp'), may hold values from -6 to 6
- short_taps: float32 [3, 3, 1024], P(None, None, 'mp'), may hold values from -3 to 3
- filter_residue: float32 [1024, 16], P('mp'), may hold values from -1.5 to 1.5
- filter_rate: float32 [1024, 16], P('mp'), may hold values from 0.00024414062 to 0.035
- hyena_skip: float32 [1024], P('mp'), may hold values from -4 to 4
Outputs:
- hyena_out: bfloat16 [2048, 1024], P('ctx', 'mp')
The draws below stay inside these ranges and needn't reach their ends.
All inputs are finite; a program needn't handle non-finite values.
Results may differ from the reference program's by a relative error of at most 0.008.
Values may be sent and summed in bfloat16 or wider, within the bound.
A program may use at most 64 MiB of HBM per device.

```python
import math
import jax
import jax.numpy as jnp
from jax import lax

CH_DEV = 256
CH = 1024
ORDER = 16
SEQ = 2048
N_MP = 4


def shard_levels(stream_key, shape, pieces, smallest, high):
    factor_of = 1.0
    for position, blocks in pieces:
        draws = jax.random.uniform(jax.random.fold_in(jax.random.fold_in(stream_key, 6), position), (blocks,), jnp.float32, smallest / len(pieces), high / len(pieces))
        factor_of = factor_of * jnp.repeat(jnp.exp(draws), shape[position] // blocks).reshape((-1,) + (1,) * (len(shape) - 1 - position))
    return factor_of


def scatter_about(stream_key, extent, deviation, most, split=(), kind=jnp.bfloat16):
    drawn = deviation * jax.random.normal(stream_key, extent, jnp.float32)
    if split:
        drawn = drawn * shard_levels(stream_key, extent, split, -0.22, 0.18)
    return jnp.clip(drawn, -most, most).astype(kind)


def setup_inputs(seed: int = 0) -> dict:
    key_of = jax.random.split(jax.random.key(seed), 6)
    return {
        "hyena_in": scatter_about(key_of[0], (3, SEQ, CH), 1.0, 6.0, ((1, 8), (2, 4))),
        "short_taps": scatter_about(key_of[1], (3, 3, CH), 0.6, 3.0, ((2, 4),), jnp.float32),
        "filter_residue": scatter_about(key_of[2], (CH, ORDER), 0.25, 1.5, ((0, 4),), jnp.float32),
        "filter_rate": jnp.clip(jnp.exp(math.log(0.035) - 4.96535895 * jax.random.uniform(key_of[3], (CH, ORDER), jnp.float32) ** shard_levels(key_of[3], (CH, ORDER), ((0, 4),), -0.2, 0.2)), 0.00024414062, 0.035),
        "hyena_skip": scatter_about(key_of[4], (CH,), 1.0, 4.0, ((0, 4),), jnp.float32),
    }


def filter_conv(block_args):
    gated_block, residue_block, rate_block = block_args
    time_steps = jnp.arange(SEQ).astype(jnp.float32)
    mode_gains = residue_block * jnp.sqrt(-jnp.expm1(-2.0 * rate_block))
    mode_values = jnp.exp(-rate_block[None, :, :] * time_steps[:, None, None])
    filter_taps = lax.optimization_barrier(jnp.sum(mode_values * mode_gains[None, :, :], axis=-1))
    padded_len = 2 * SEQ
    spectrum = jnp.fft.rfft(filter_taps, n=padded_len, axis=0) * jnp.fft.rfft(gated_block, n=padded_len, axis=0)
    return jnp.fft.irfft(spectrum, n=padded_len, axis=0)[:SEQ]

def reference(hyena_in, short_taps, filter_residue, filter_rate, hyena_skip):
    inputs = hyena_in.astype(jnp.float32)
    padded = jnp.pad(inputs, ((0, 0), (2, 0), (0, 0)))
    shorted = short_taps[:, 0, None, :] * padded[:, 2:, :] + short_taps[:, 1, None, :] * padded[:, 1:-1, :] + short_taps[:, 2, None, :] * padded[:, :-2, :]
    gated_signal = shorted[1] * shorted[2]
    gated_blocks = gated_signal.reshape(SEQ, N_MP, CH_DEV).transpose(1, 0, 2)
    residue_blocks = filter_residue.reshape(N_MP, CH_DEV, ORDER)
    rate_blocks = filter_rate.reshape(N_MP, CH_DEV, ORDER)
    conv_blocks = lax.map(filter_conv, (gated_blocks, residue_blocks, rate_blocks))
    convolved = conv_blocks.transpose(1, 0, 2).reshape(SEQ, CH)
    return (shorted[0] * (convolved + hyena_skip * gated_signal)).astype(jnp.bfloat16)
```

```python
import functools

import jax
import jax.numpy as jnp
from jax import lax
from jax.experimental import pallas as pl
from jax.experimental.pallas import tpu as pltpu
from jax.sharding import PartitionSpec as P

MESH = pl.DeviceIdType.MESH
SUBS = 8
LANES = 128
EDGE_ROWS = 16
TAIL = {0: 0, 1: 2, 2: 4}
HEAD = {1: 6, 2: 8}


def kernel(
    count, x_hbm, taps_hbm, res_hbm, rate_hbm, skip_hbm, out_ref,
    xb, xf, taps, res, rate, skip, ub, sb, yb, of, packed, outbox, inbox, excl, far, entry,
    load_sems, send_sems, recv_sems,
):
    me = lax.axis_index("ctx")
    rows, channels = out_ref.shape
    order = rate.shape[0]
    steps = rows // SUBS

    barrier = pltpu.get_barrier_semaphore()
    for d in range(1, count):
        @pl.when(me >= d)
        def _():
            pl.semaphore_signal(
                barrier, inc=1, device_id={"ctx": lax.rem(me - d + count, count)},
                device_id_type=MESH,
            )

    loads = [
        pltpu.make_async_copy(source, target, load_sems.at[i])
        for i, (source, target) in enumerate(
            [(rate_hbm, rate), (res_hbm, res), (taps_hbm, taps), (skip_hbm, skip), (x_hbm, xb)]
        )
    ]
    for load in reversed(loads):
        load.start()

    for d in range(1, count):
        @pl.when(me < d)
        def _():
            inbox[d - 1] = jnp.zeros(inbox.shape[1:], inbox.dtype)

    sub = lax.broadcasted_iota(jnp.int32, (SUBS, LANES), 0)
    for load in loads:
        load.wait()

    mode_rate = rate[...]
    decay = jnp.exp(-mode_rate)
    grow = jnp.exp(mode_rate)
    hyper = jnp.tanh(mode_rate)
    gain = res[...] * jnp.sqrt(2.0 * hyper / (1.0 + hyper))
    span1 = jnp.exp(-steps * mode_rate)
    span2 = span1 * span1
    span4 = span2 * span2
    block_decay = span4 * span4
    ahead = jnp.sum(gain * grow, axis=0, keepdims=True)

    packed[...] = jnp.zeros_like(packed)
    for lane in range(0, channels, LANES):
        ln = pl.ds(lane, LANES)
        tile = lane // LANES
        for p in range(3):
            xf[p, tile] = xb[p, :, ln].astype(jnp.float32)
        for p, row in TAIL.items():
            packed[order + row : order + row + 2, ln] = xf[p, tile, rows - 2 : rows, :]
        for p, row in HEAD.items():
            packed[order + row : order + row + 2, ln] = xf[p, tile, 0:2, :]

    def spread(table, r, lane):
        return jnp.broadcast_to(table[r : r + 1, lane : lane + LANES], (SUBS, LANES))

    for lane in range(0, channels, LANES):
        ln = pl.ds(lane, LANES)
        weight = [
            [jnp.broadcast_to(taps[p, l : l + 1, ln], (SUBS, LANES)) for l in range(3)]
            for p in range(3)
        ]
        a = [spread(decay, r, lane) for r in range(order)]

        def before(p, k):
            last = xf[p, lane // LANES, pl.ds(k, SUBS, stride=steps), :]
            return jnp.where(sub == 0, 0.0, pltpu.roll(last, 1, 0))

        def gate(k, carry):
            prev1, prev2, h = carry
            now = [xf[p, lane // LANES, pl.ds(k, SUBS, stride=steps), :] for p in range(3)]
            s = [
                weight[p][0] * now[p] + weight[p][1] * prev1[p] + weight[p][2] * prev2[p]
                for p in range(3)
            ]
            u = jnp.where((sub == 0) & (k < 2), 0.0, s[1] * s[2])
            ub[k, :, ln] = u
            sb[k, :, ln] = s[0]
            return now, prev1, [a[r] * h[r] + u for r in range(order)]

        start = (
            [before(p, steps - 1) for p in range(3)],
            [before(p, steps - 2) for p in range(3)],
            [jnp.zeros((SUBS, LANES), jnp.float32)] * order,
        )
        _, _, h = lax.fori_loop(0, steps, gate, start, unroll=4)
        for r in range(order):
            total = h[r]
            for shift, table in ((1, span1), (2, span2), (4, span4)):
                total = total + jnp.where(
                    sub >= shift, spread(table, r, lane) * pltpu.roll(total, shift, 0), 0.0
                )
            packed[r : r + 1, ln] = total[SUBS - 1 : SUBS, :]
            excl[r, :, ln] = jnp.where(sub >= 1, pltpu.roll(total, 1, 0), 0.0)

    outbox[...] = packed[...].astype(outbox.dtype)

    @pl.when(me < count - 1)
    def _():
        pl.semaphore_wait(barrier, count - 1 - me)

    copies = [
        pltpu.make_async_remote_copy(
            src_ref=outbox,
            dst_ref=inbox.at[d - 1],
            send_sem=send_sems.at[d - 1],
            recv_sem=recv_sems.at[d - 1],
            device_id={"ctx": lax.rem(me + d, count)},
            device_id_type=MESH,
        )
        for d in range(1, count)
    ]
    for d in range(1, count):
        @pl.when(me + d < count)
        def _():
            copies[d - 1].start()

    for lane in range(0, channels, LANES):
        ln = pl.ds(lane, LANES)
        a = [spread(decay, r, lane) for r in range(order)]
        g = [spread(gain, r, lane) for r in range(order)]
        direct = jnp.broadcast_to(skip[0:1, ln], (SUBS, LANES))

        def local(k, h):
            u = ub[k, :, ln]
            h = [a[r] * h[r] + u for r in range(order)]
            terms = [g[r] * h[r] for r in range(order)] + [direct * u]
            while len(terms) > 1:
                terms = [sum(terms[i : i + 2]) for i in range(0, len(terms), 2)]
            yb[k, :, ln] = terms[0]
            return h

        lax.fori_loop(0, steps, local, [excl[r, :, ln] for r in range(order)], unroll=4)
        for r in range(order):
            distance = (sub * steps).astype(jnp.float32)
            far[r, :, ln] = g[r] * jnp.exp(-spread(mode_rate, r, lane) * distance)

    for d in range(1, count):
        @pl.when(me >= d)
        def _():
            copies[d - 1].wait_recv()

    def gated_head(heads, tails):
        s = []
        for p in (1, 2):
            x0, x1 = (heads[HEAD[p] + i : HEAD[p] + i + 1] for i in range(2))
            t2, t1 = (tails[TAIL[p] + i : TAIL[p] + i + 1] for i in range(2))
            w0, w1, w2 = (taps[p, l : l + 1, :] for l in range(3))
            s.append((w0 * x0 + w1 * t1 + w2 * t2, w0 * x1 + w1 * x0 + w2 * t1))
        return s[0][0] * s[1][0], s[0][1] * s[1][1]

    carried = jnp.zeros((order, channels), jnp.float32)
    tails = jnp.zeros((EDGE_ROWS, channels), jnp.float32)
    for d in range(count - 1, 0, -1):
        packet = inbox[d - 1].astype(jnp.float32)
        edges = packet[order:, :]
        u0, u1 = gated_head(edges, tails)
        carried = block_decay * (carried + grow * (u0 + grow * u1)) + packet[:order, :]
        tails = edges
    u0, u1 = gated_head(packed[order:, :], tails)
    entry[...] = carried + grow * (u0 + grow * u1)
    yb[0, 0:1, :] = yb[0, 0:1, :] + skip[...] * u0 - ahead * u1
    yb[1, 0:1, :] = yb[1, 0:1, :] + skip[...] * u1
    sb[0, 0:1, :] = sb[0, 0:1, :] + taps[0, 1:2, :] * tails[1:2] + taps[0, 2:3, :] * tails[0:1]
    sb[1, 0:1, :] = sb[1, 0:1, :] + taps[0, 2:3, :] * tails[1:2]

    for lane in range(0, channels, LANES):
        ln = pl.ds(lane, LANES)
        a = [spread(decay, r, lane) for r in range(order)]

        def finish(k, e):
            e = [a[r] * e[r] for r in range(order)]
            terms = e
            while len(terms) > 1:
                terms = [sum(terms[i : i + 2]) for i in range(0, len(terms), 2)]
            of[lane // LANES, pl.ds(k, SUBS, stride=steps), :] = sb[k, :, ln] * (yb[k, :, ln] + terms[0])
            return e

        first = [far[r, :, ln] * jnp.broadcast_to(entry[r : r + 1, ln], (SUBS, LANES)) for r in range(order)]
        lax.fori_loop(0, steps, finish, first, unroll=4)

        out_ref[:, ln] = of[lane // LANES].astype(out_ref.dtype)

    for d in range(1, count):
        @pl.when(me + d < count)
        def _():
            copies[d - 1].wait_send()


def body(hyena_in, short_taps, filter_residue, filter_rate, hyena_skip):
    count = lax.axis_size("ctx")
    _, rows, channels = hyena_in.shape
    order = filter_rate.shape[1]
    steps = rows // SUBS
    f32, bf16 = jnp.float32, jnp.bfloat16
    packet = order + EDGE_ROWS
    return pl.pallas_call(
        functools.partial(kernel, count),
        out_shape=jax.ShapeDtypeStruct((rows, channels), bf16),
        in_specs=[pl.BlockSpec(memory_space=pl.ANY)] * 5,
        out_specs=pl.BlockSpec(memory_space=pltpu.VMEM),
        scratch_shapes=[
            pltpu.VMEM((3, rows, channels), bf16),
            pltpu.VMEM((3, channels // LANES, rows, LANES), f32),
            pltpu.VMEM((3, 3, channels), f32),
            pltpu.VMEM((order, channels), f32),
            pltpu.VMEM((order, channels), f32),
            pltpu.VMEM((1, channels), f32),
            pltpu.VMEM((steps, SUBS, channels), f32),
            pltpu.VMEM((steps, SUBS, channels), f32),
            pltpu.VMEM((steps, SUBS, channels), f32),
            pltpu.VMEM((channels // LANES, rows, LANES), f32),
            pltpu.VMEM((packet, channels), f32),
            pltpu.VMEM((packet, channels), bf16),
            pltpu.VMEM((count - 1, packet, channels), bf16),
            pltpu.VMEM((order, SUBS, channels), f32),
            pltpu.VMEM((order, SUBS, channels), f32),
            pltpu.VMEM((order, channels), f32),
            pltpu.SemaphoreType.DMA((5,)),
            pltpu.SemaphoreType.DMA((count - 1,)),
            pltpu.SemaphoreType.DMA((count - 1,)),
        ],
        compiler_params=pltpu.CompilerParams(collective_id=0, has_side_effects=True),
    )(hyena_in, short_taps, filter_residue.T, filter_rate.T, hyena_skip.reshape(1, channels))


def solution(mesh):
    return jax.shard_map(
        body,
        mesh=mesh,
        in_specs=(P(None, "ctx", "mp"), P(None, None, "mp"), P("mp", None), P("mp", None), P("mp")),
        out_specs=P("ctx", "mp"),
        check_vma=False,
    )
```

```python
import functools

import jax
import jax.numpy as jnp
from jax import lax
from jax.experimental import pallas as pl
from jax.experimental.pallas import tpu as pltpu
from jax.sharding import PartitionSpec as P

MESH = pl.DeviceIdType.MESH
SUBS = 8
LANES = 128
EDGE_ROWS = 16
TAIL = {0: 0, 1: 2, 2: 4}
HEAD = {1: 6, 2: 8}


def add_up(terms):
    while len(terms) > 1:
        pairs = [terms[i] + terms[i + 1] for i in range(0, len(terms) - 1, 2)]
        terms = pairs + terms[2 * len(pairs) :]
    return terms[0]


def exchange(
    count, x_hbm, taps_hbm, res_hbm, rate_hbm, skip_hbm, yb, sb, modes, decays,
    xb, xf, taps, res, rate, skip, ub, packed, outbox, inbox, excl, far, impulse,
    load_sems, x_sems, send_sems, recv_sems,
):
    me = lax.axis_index("ctx")
    tiles = xf.shape[1]
    rows, channels = xf.shape[2], tiles * LANES
    order = rate.shape[0]
    steps = rows // SUBS

    barrier = pltpu.get_barrier_semaphore()
    for d in range(1, count):
        @pl.when(me >= d)
        def _():
            pl.semaphore_signal(
                barrier, inc=1, device_id={"ctx": lax.rem(me - d + count, count)},
                device_id_type=MESH,
            )

    loads = [
        pltpu.make_async_copy(source, target, load_sems.at[i])
        for i, (source, target) in enumerate(
            [(rate_hbm, rate), (res_hbm, res), (taps_hbm, taps), (skip_hbm, skip)]
        )
    ]
    for load in loads:
        load.start()
    streams = []
    for tile in range(tiles):
        ln = pl.ds(tile * LANES, LANES)
        streams.append([
            pltpu.make_async_copy(x_hbm.at[p, :, ln], xb.at[p, tile], x_sems.at[p, tile])
            for p in range(3)
        ])
        for load in streams[tile]:
            load.start()

    for d in range(1, count):
        @pl.when(me < d)
        def _():
            inbox[d - 1] = jnp.zeros(inbox.shape[1:], inbox.dtype)

    packed[...] = jnp.zeros_like(packed)
    sub = lax.broadcasted_iota(jnp.int32, (SUBS, LANES), 0)
    for load in loads:
        load.wait()

    mode_rate = rate[...]
    decay = jnp.exp(-mode_rate)
    decays[...] = decay
    grow = jnp.exp(mode_rate)
    hyper = jnp.tanh(mode_rate)
    gain = res[...] * jnp.sqrt(2.0 * hyper / (1.0 + hyper))
    span1 = jnp.exp(-steps * mode_rate)
    span2 = span1 * span1
    span4 = span2 * span2
    block_decay = span4 * span4
    ahead = jnp.sum(gain * grow, axis=0, keepdims=True)

    def spread(table, r, lane, height=SUBS):
        return jnp.broadcast_to(table[r : r + 1, lane : lane + LANES], (height, LANES))

    for tile in range(tiles):
        lane = tile * LANES
        ln = pl.ds(lane, LANES)
        for p in range(3):
            streams[tile][p].wait()
            xf[p, tile] = xb[p, tile].astype(jnp.float32)
        for p, row in TAIL.items():
            packed[order + row : order + row + 2, ln] = xf[p, tile, rows - 2 : rows, :]
        for p, row in HEAD.items():
            packed[order + row : order + row + 2, ln] = xf[p, tile, 0:2, :]
        weight = [
            [jnp.broadcast_to(taps[p, l : l + 1, ln], (SUBS, LANES)) for l in range(3)]
            for p in range(3)
        ]
        a = [spread(decay, r, lane) for r in range(order)]

        def before(p, k):
            last = xf[p, tile, pl.ds(k, SUBS, stride=steps), :]
            return jnp.where(sub == 0, 0.0, pltpu.roll(last, 1, 0))

        def gate(k, carry):
            prev1, prev2, h = carry
            now = [xf[p, tile, pl.ds(k, SUBS, stride=steps), :] for p in range(3)]
            s = [
                weight[p][0] * now[p] + weight[p][1] * prev1[p] + weight[p][2] * prev2[p]
                for p in range(3)
            ]
            u = jnp.where((sub == 0) & (k < 2), 0.0, s[1] * s[2])
            ub[k, :, ln] = u
            sb[k, :, ln] = s[0]
            return now, prev1, [a[r] * h[r] + u for r in range(order)]

        start = (
            [before(p, steps - 1) for p in range(3)],
            [before(p, steps - 2) for p in range(3)],
            [jnp.zeros((SUBS, LANES), jnp.float32)] * order,
        )
        _, _, h = lax.fori_loop(0, steps, gate, start, unroll=4)
        for r in range(order):
            total = h[r]
            for shift, table in ((1, span1), (2, span2), (4, span4)):
                total = total + jnp.where(
                    sub >= shift, spread(table, r, lane) * pltpu.roll(total, shift, 0), 0.0
                )
            packed[r : r + 1, ln] = total[SUBS - 1 : SUBS, :]
            excl[r, :, ln] = jnp.where(sub >= 1, pltpu.roll(total, 1, 0), 0.0)

    outbox[...] = packed[...].astype(outbox.dtype)

    @pl.when(me < count - 1)
    def _():
        pl.semaphore_wait(barrier, count - 1 - me)

    copies = [
        pltpu.make_async_remote_copy(
            src_ref=outbox,
            dst_ref=inbox.at[d - 1],
            send_sem=send_sems.at[d - 1],
            recv_sem=recv_sems.at[d - 1],
            device_id={"ctx": lax.rem(me + d, count)},
            device_id_type=MESH,
        )
        for d in range(1, count)
    ]
    for d in range(1, count):
        @pl.when(me + d < count)
        def _():
            copies[d - 1].start()

    for tile in range(tiles):
        lane = tile * LANES
        ln = pl.ds(lane, LANES)
        time = lax.broadcasted_iota(jnp.int32, (steps, LANES), 0).astype(jnp.float32)
        response = add_up([
            spread(gain, r, lane, steps) * jnp.exp(-spread(mode_rate, r, lane, steps) * time)
            for r in range(order)
        ])
        impulse[:, ln] = response
        impulse[0:1, ln] = response[0:1, :] + skip[0:1, ln]
        for first in range(0, steps, SUBS):
            total = [None] * SUBS
            for lag in range(0, first + 1, SUBS):
                source = first - lag
                u = [ub[source + i, :, ln] for i in range(SUBS)]
                for delay in range(max(0, lag - SUBS + 1), lag + SUBS):
                    tap = jnp.broadcast_to(impulse[delay : delay + 1, ln], (SUBS, LANES))
                    for i in range(SUBS):
                        k = source + i + delay - first
                        if 0 <= k < SUBS:
                            term = tap * u[i]
                            total[k] = term if total[k] is None else total[k] + term
            for k in range(SUBS):
                yb[first + k, :, ln] = total[k]
        distance = (sub * steps).astype(jnp.float32)
        for r in range(order):
            g = spread(gain, r, lane)
            far[r, :, ln] = g * jnp.exp(-spread(mode_rate, r, lane) * distance)
            excl[r, :, ln] = g * excl[r, :, ln]

    for d in range(1, count):
        @pl.when(me >= d)
        def _():
            copies[d - 1].wait_recv()

    def gated_head(heads, tails):
        s = []
        for p in (1, 2):
            x0, x1 = (heads[HEAD[p] + i : HEAD[p] + i + 1] for i in range(2))
            t2, t1 = (tails[TAIL[p] + i : TAIL[p] + i + 1] for i in range(2))
            w0, w1, w2 = (taps[p, l : l + 1, :] for l in range(3))
            s.append((w0 * x0 + w1 * t1 + w2 * t2, w0 * x1 + w1 * x0 + w2 * t1))
        return s[0][0] * s[1][0], s[0][1] * s[1][1]

    carried = jnp.zeros((order, channels), jnp.float32)
    tails = jnp.zeros((EDGE_ROWS, channels), jnp.float32)
    for d in range(count - 1, 0, -1):
        packet = inbox[d - 1].astype(jnp.float32)
        edges = packet[order:, :]
        u0, u1 = gated_head(edges, tails)
        carried = block_decay * (carried + grow * (u0 + grow * u1)) + packet[:order, :]
        tails = edges
    u0, u1 = gated_head(packed[order:, :], tails)
    entry = carried + grow * (u0 + grow * u1)
    for lane in range(0, channels, LANES):
        ln = pl.ds(lane, LANES)
        for r in range(order):
            modes[r, :, ln] = excl[r, :, ln] + far[r, :, ln] * spread(entry, r, lane)
    yb[0, 0:1, :] = yb[0, 0:1, :] + skip[...] * u0 - ahead * u1
    yb[1, 0:1, :] = yb[1, 0:1, :] + skip[...] * u1
    sb[0, 0:1, :] = sb[0, 0:1, :] + taps[0, 1:2, :] * tails[1:2] + taps[0, 2:3, :] * tails[0:1]
    sb[1, 0:1, :] = sb[1, 0:1, :] + taps[0, 2:3, :] * tails[1:2]

    for d in range(1, count):
        @pl.when(me + d < count)
        def _():
            copies[d - 1].wait_send()


def finish(yb, sb, modes, decays, out_hbm, of, ob, sems):
    steps, _, channels = yb.shape
    order = modes.shape[0]
    stores = []
    for tile in range(channels // LANES):
        ln = pl.ds(tile * LANES, LANES)
        a = [jnp.broadcast_to(decays[r : r + 1, ln], (SUBS, LANES)) for r in range(order)]

        def step(k, e):
            e = [a[r] * e[r] for r in range(order)]
            of[tile, pl.ds(k, SUBS, stride=steps), :] = sb[k, :, ln] * (yb[k, :, ln] + add_up(e))
            return e

        lax.fori_loop(0, steps, step, [modes[r, :, ln] for r in range(order)], unroll=4)
        ob[tile] = of[tile].astype(ob.dtype)
        stores.append(pltpu.make_async_copy(ob.at[tile], out_hbm.at[:, ln], sems.at[tile]))
        stores[tile].start()
    for store in stores:
        store.wait()


def body(hyena_in, short_taps, filter_residue, filter_rate, hyena_skip):
    count = lax.axis_size("ctx")
    _, rows, channels = hyena_in.shape
    order = filter_rate.shape[1]
    steps, tiles = rows // SUBS, channels // LANES
    f32, bf16 = jnp.float32, jnp.bfloat16
    packet = order + EDGE_ROWS
    signal = jax.ShapeDtypeStruct((steps, SUBS, channels), f32)
    states = jax.ShapeDtypeStruct((order, SUBS, channels), f32)
    table = jax.ShapeDtypeStruct((order, channels), f32)
    vmem = pl.BlockSpec(memory_space=pltpu.VMEM)
    parts = pl.pallas_call(
        functools.partial(exchange, count),
        out_shape=[signal, signal, states, table],
        in_specs=[pl.BlockSpec(memory_space=pltpu.HBM)] * 5,
        out_specs=[vmem] * 4,
        scratch_shapes=[
            pltpu.VMEM((3, tiles, rows, LANES), bf16),
            pltpu.VMEM((3, tiles, rows, LANES), f32),
            pltpu.VMEM((3, 3, channels), f32),
            pltpu.VMEM((order, channels), f32),
            pltpu.VMEM((order, channels), f32),
            pltpu.VMEM((1, channels), f32),
            pltpu.VMEM((steps, SUBS, channels), f32),
            pltpu.VMEM((packet, channels), f32),
            pltpu.VMEM((packet, channels), bf16),
            pltpu.VMEM((count - 1, packet, channels), bf16),
            pltpu.VMEM((order, SUBS, channels), f32),
            pltpu.VMEM((order, SUBS, channels), f32),
            pltpu.VMEM((steps, channels), f32),
            pltpu.SemaphoreType.DMA((4,)),
            pltpu.SemaphoreType.DMA((3, tiles)),
            pltpu.SemaphoreType.DMA((count - 1,)),
            pltpu.SemaphoreType.DMA((count - 1,)),
        ],
        compiler_params=pltpu.CompilerParams(
            collective_id=0, has_side_effects=True, vmem_limit_bytes=8 << 20
        ),
    )(hyena_in, short_taps, filter_residue.T, filter_rate.T, hyena_skip.reshape(1, channels))
    return pl.pallas_call(
        finish,
        out_shape=jax.ShapeDtypeStruct((rows, channels), bf16),
        in_specs=[vmem] * 4,
        out_specs=pl.BlockSpec(memory_space=pltpu.HBM),
        scratch_shapes=[
            pltpu.VMEM((tiles, rows, LANES), f32),
            pltpu.VMEM((tiles, rows, LANES), bf16),
            pltpu.SemaphoreType.DMA((tiles,)),
        ],
        compiler_params=pltpu.CompilerParams(vmem_limit_bytes=8 << 20),
    )(*parts)


def solution(mesh):
    return jax.shard_map(
        body,
        mesh=mesh,
        in_specs=(P(None, "ctx", "mp"), P(None, None, "mp"), P("mp", None), P("mp", None), P("mp")),
        out_specs=P("ctx", "mp"),
        check_vma=False,
    )
```

```python
import functools

import jax
import jax.numpy as jnp
from jax import lax
from jax.experimental import pallas as pl
from jax.experimental.pallas import tpu as pltpu
from jax.sharding import PartitionSpec as P

MESH = pl.DeviceIdType.MESH
SUBS = 8
LANES = 128
EDGE_ROWS = 16
TAIL = {0: 0, 1: 2, 2: 4}
HEAD = {1: 6, 2: 8}


def add_up(terms):
    while len(terms) > 1:
        pairs = [terms[i] + terms[i + 1] for i in range(0, len(terms) - 1, 2)]
        terms = pairs + terms[2 * len(pairs) :]
    return terms[0]


def exchange(
    count, x_hbm, taps_hbm, res_hbm, rate_hbm, skip_hbm, yb, sb, modes, decays,
    xb, xf, taps, res, rate, skip, ub, packed, outbox, inbox, excl, far, impulse,
    load_sems, x_sems, send_sems, recv_sems,
):
    me = lax.axis_index("ctx")
    tiles = xf.shape[1]
    rows, channels = xf.shape[2], tiles * LANES
    order = rate.shape[0]
    steps = rows // SUBS

    barrier = pltpu.get_barrier_semaphore()
    for d in range(1, count):
        @pl.when(me >= d)
        def _():
            pl.semaphore_signal(
                barrier, inc=1, device_id={"ctx": lax.rem(me - d + count, count)},
                device_id_type=MESH,
            )

    loads = [
        pltpu.make_async_copy(source, target, load_sems.at[i])
        for i, (source, target) in enumerate(
            [(rate_hbm, rate), (res_hbm, res), (taps_hbm, taps), (skip_hbm, skip)]
        )
    ]
    for load in loads:
        load.start()
    streams = []
    for tile in range(tiles):
        ln = pl.ds(tile * LANES, LANES)
        streams.append([
            pltpu.make_async_copy(x_hbm.at[p, :, ln], xb.at[p, tile], x_sems.at[p, tile])
            for p in range(3)
        ])
        for load in streams[tile]:
            load.start()

    for d in range(1, count):
        @pl.when(me < d)
        def _():
            inbox[d - 1] = jnp.zeros(inbox.shape[1:], inbox.dtype)

    packed[...] = jnp.zeros_like(packed)
    sub = lax.broadcasted_iota(jnp.int32, (SUBS, LANES), 0)
    for load in loads:
        load.wait()

    mode_rate = rate[...]
    decay = jnp.exp(-mode_rate)
    decays[...] = decay
    grow = jnp.exp(mode_rate)
    hyper = jnp.tanh(mode_rate)
    gain = res[...] * jnp.sqrt(2.0 * hyper / (1.0 + hyper))
    span1 = jnp.exp(-steps * mode_rate)
    span2 = span1 * span1
    span4 = span2 * span2
    block_decay = span4 * span4
    ahead = jnp.sum(gain * grow, axis=0, keepdims=True)

    def spread(table, r, lane, height=SUBS):
        return jnp.broadcast_to(table[r : r + 1, lane : lane + LANES], (height, LANES))

    for tile in range(tiles):
        lane = tile * LANES
        ln = pl.ds(lane, LANES)
        for p in range(3):
            streams[tile][p].wait()
            xf[p, tile] = xb[p, tile].astype(jnp.float32)
        for p, row in TAIL.items():
            packed[order + row : order + row + 2, ln] = xf[p, tile, rows - 2 : rows, :]
        for p, row in HEAD.items():
            packed[order + row : order + row + 2, ln] = xf[p, tile, 0:2, :]
        weight = [
            [jnp.broadcast_to(taps[p, l : l + 1, ln], (SUBS, LANES)) for l in range(3)]
            for p in range(3)
        ]
        a = [spread(decay, r, lane) for r in range(order)]

        def before(p, k):
            last = xf[p, tile, pl.ds(k, SUBS, stride=steps), :]
            return jnp.where(sub == 0, 0.0, pltpu.roll(last, 1, 0))

        def gate(k, carry):
            prev1, prev2, h = carry
            now = [xf[p, tile, pl.ds(k, SUBS, stride=steps), :] for p in range(3)]
            s = [
                weight[p][0] * now[p] + weight[p][1] * prev1[p] + weight[p][2] * prev2[p]
                for p in range(3)
            ]
            u = jnp.where((sub == 0) & (k < 2), 0.0, s[1] * s[2])
            ub[k, :, ln] = u
            sb[k, :, ln] = s[0]
            return now, prev1, [a[r] * h[r] + u for r in range(order)]

        start = (
            [before(p, steps - 1) for p in range(3)],
            [before(p, steps - 2) for p in range(3)],
            [jnp.zeros((SUBS, LANES), jnp.float32)] * order,
        )
        _, _, h = lax.fori_loop(0, steps, gate, start, unroll=4)
        for r in range(order):
            total = h[r]
            for shift, table in ((1, span1), (2, span2), (4, span4)):
                total = total + jnp.where(
                    sub >= shift, spread(table, r, lane) * pltpu.roll(total, shift, 0), 0.0
                )
            packed[r : r + 1, ln] = total[SUBS - 1 : SUBS, :]
            excl[r, :, ln] = jnp.where(sub >= 1, pltpu.roll(total, 1, 0), 0.0)

    outbox[...] = packed[...].astype(outbox.dtype)

    @pl.when(me < count - 1)
    def _():
        pl.semaphore_wait(barrier, count - 1 - me)

    copies = [
        pltpu.make_async_remote_copy(
            src_ref=outbox,
            dst_ref=inbox.at[d - 1],
            send_sem=send_sems.at[d - 1],
            recv_sem=recv_sems.at[d - 1],
            device_id={"ctx": lax.rem(me + d, count)},
            device_id_type=MESH,
        )
        for d in range(1, count)
    ]
    for d in range(1, count):
        @pl.when(me + d < count)
        def _():
            copies[d - 1].start()

    for tile in range(tiles):
        lane = tile * LANES
        ln = pl.ds(lane, LANES)
        time = lax.broadcasted_iota(jnp.int32, (steps, LANES), 0).astype(jnp.float32)
        response = add_up([
            spread(gain, r, lane, steps) * jnp.exp(-spread(mode_rate, r, lane, steps) * time)
            for r in range(order)
        ])
        impulse[:, ln] = response
        impulse[0:1, ln] = response[0:1, :] + skip[0:1, ln]
        for first in range(0, steps, SUBS):
            total = [None] * SUBS
            for lag in range(0, first + 1, SUBS):
                source = first - lag
                u = [ub[source + i, :, ln] for i in range(SUBS)]
                for delay in range(max(0, lag - SUBS + 1), lag + SUBS):
                    tap = jnp.broadcast_to(impulse[delay : delay + 1, ln], (SUBS, LANES))
                    for i in range(SUBS):
                        k = source + i + delay - first
                        if 0 <= k < SUBS:
                            term = tap * u[i]
                            total[k] = term if total[k] is None else total[k] + term
            for k in range(SUBS):
                yb[first + k, :, ln] = total[k]
        distance = (sub * steps).astype(jnp.float32)
        for r in range(order):
            g = spread(gain, r, lane)
            far[r, :, ln] = g * jnp.exp(-spread(mode_rate, r, lane) * distance)
            excl[r, :, ln] = g * excl[r, :, ln]

    for d in range(1, count):
        @pl.when(me >= d)
        def _():
            copies[d - 1].wait_recv()

    def gated_head(heads, tails):
        s = []
        for p in (1, 2):
            x0, x1 = (heads[HEAD[p] + i : HEAD[p] + i + 1] for i in range(2))
            t2, t1 = (tails[TAIL[p] + i : TAIL[p] + i + 1] for i in range(2))
            w0, w1, w2 = (taps[p, l : l + 1, :] for l in range(3))
            s.append((w0 * x0 + w1 * t1 + w2 * t2, w0 * x1 + w1 * x0 + w2 * t1))
        return s[0][0] * s[1][0], s[0][1] * s[1][1]

    carried = jnp.zeros((order, channels), jnp.float32)
    tails = jnp.zeros((EDGE_ROWS, channels), jnp.float32)
    for d in range(count - 1, 0, -1):
        packet = inbox[d - 1].astype(jnp.float32)
        edges = packet[order:, :]
        u0, u1 = gated_head(edges, tails)
        carried = block_decay * (carried + grow * (u0 + grow * u1)) + packet[:order, :]
        tails = edges
    u0, u1 = gated_head(packed[order:, :], tails)
    entry = carried + grow * (u0 + grow * u1)
    for lane in range(0, channels, LANES):
        ln = pl.ds(lane, LANES)
        for r in range(order):
            modes[r, :, ln] = excl[r, :, ln] + far[r, :, ln] * spread(entry, r, lane)
    yb[0, 0:1, :] = yb[0, 0:1, :] + skip[...] * u0 - ahead * u1
    yb[1, 0:1, :] = yb[1, 0:1, :] + skip[...] * u1
    sb[0, 0:1, :] = sb[0, 0:1, :] + taps[0, 1:2, :] * tails[1:2] + taps[0, 2:3, :] * tails[0:1]
    sb[1, 0:1, :] = sb[1, 0:1, :] + taps[0, 2:3, :] * tails[1:2]

    for d in range(1, count):
        @pl.when(me + d < count)
        def _():
            copies[d - 1].wait_send()


def finish(yb, sb, modes, decays, out_hbm, of, ob, sems):
    steps, _, channels = yb.shape
    order = modes.shape[0]
    stores = []
    for tile in range(channels // LANES):
        ln = pl.ds(tile * LANES, LANES)
        a = [jnp.broadcast_to(decays[r : r + 1, ln], (SUBS, LANES)) for r in range(order)]

        def step(k, e):
            e = [a[r] * e[r] for r in range(order)]
            of[tile, pl.ds(k, SUBS, stride=steps), :] = sb[k, :, ln] * (yb[k, :, ln] + add_up(e))
            return e

        lax.fori_loop(0, steps, step, [modes[r, :, ln] for r in range(order)], unroll=4)
        ob[tile] = of[tile].astype(ob.dtype)
        stores.append(pltpu.make_async_copy(ob.at[tile], out_hbm.at[:, ln], sems.at[tile]))
        stores[tile].start()
    for store in stores:
        store.wait()


def body(hyena_in, short_taps, filter_residue, filter_rate, hyena_skip):
    count = lax.axis_size("ctx")
    _, rows, channels = hyena_in.shape
    order = filter_rate.shape[1]
    steps, tiles = rows // SUBS, channels // LANES
    f32, bf16 = jnp.float32, jnp.bfloat16
    packet = order + EDGE_ROWS
    signal = jax.ShapeDtypeStruct((steps, SUBS, channels), f32)
    states = jax.ShapeDtypeStruct((order, SUBS, channels), f32)
    table = jax.ShapeDtypeStruct((order, channels), f32)
    vmem = pl.BlockSpec(memory_space=pltpu.VMEM)
    parts = pl.pallas_call(
        functools.partial(exchange, count),
        out_shape=[signal, signal, states, table],
        in_specs=[pl.BlockSpec(memory_space=pltpu.HBM)] * 5,
        out_specs=[vmem] * 4,
        scratch_shapes=[
            pltpu.VMEM((3, tiles, rows, LANES), bf16),
            pltpu.VMEM((3, tiles, rows, LANES), f32),
            pltpu.VMEM((3, 3, channels), f32),
            pltpu.VMEM((order, channels), f32),
            pltpu.VMEM((order, channels), f32),
            pltpu.VMEM((1, channels), f32),
            pltpu.VMEM((steps, SUBS, channels), f32),
            pltpu.VMEM((packet, channels), f32),
            pltpu.VMEM((packet, channels), bf16),
            pltpu.VMEM((count - 1, packet, channels), bf16),
            pltpu.VMEM((order, SUBS, channels), f32),
            pltpu.VMEM((order, SUBS, channels), f32),
            pltpu.VMEM((steps, channels), f32),
            pltpu.SemaphoreType.DMA((4,)),
            pltpu.SemaphoreType.DMA((3, tiles)),
            pltpu.SemaphoreType.DMA((count - 1,)),
            pltpu.SemaphoreType.DMA((count - 1,)),
        ],
        compiler_params=pltpu.CompilerParams(
            collective_id=0, has_side_effects=True, vmem_limit_bytes=8 << 20
        ),
    )(*(
        pltpu.with_memory_space_constraint(value, pltpu.HBM)
        for value in (
            hyena_in, short_taps, filter_residue.T, filter_rate.T, hyena_skip.reshape(1, channels)
        )
    ))
    return pl.pallas_call(
        finish,
        out_shape=jax.ShapeDtypeStruct((rows, channels), bf16),
        in_specs=[vmem] * 4,
        out_specs=pl.BlockSpec(memory_space=pltpu.HBM),
        scratch_shapes=[
            pltpu.VMEM((tiles, rows, LANES), f32),
            pltpu.VMEM((tiles, rows, LANES), bf16),
            pltpu.SemaphoreType.DMA((tiles,)),
        ],
        compiler_params=pltpu.CompilerParams(vmem_limit_bytes=8 << 20),
    )(*parts)


def solution(mesh):
    return jax.shard_map(
        body,
        mesh=mesh,
        in_specs=(P(None, "ctx", "mp"), P(None, None, "mp"), P("mp", None), P("mp", None), P("mp")),
        out_specs=P("ctx", "mp"),
        check_vma=False,
    )
```

```python
import functools

import jax
import jax.numpy as jnp
from jax import lax
from jax.experimental import pallas as pl
from jax.experimental.pallas import tpu as pltpu
from jax.sharding import PartitionSpec as P

MESH = pl.DeviceIdType.MESH
SUBS = 8
LANES = 128


def add_up(terms):
    while len(terms) > 1:
        pairs = [terms[i] + terms[i + 1] for i in range(0, len(terms) - 1, 2)]
        terms = pairs + terms[2 * len(pairs) :]
    return terms[0]


def exchange(
    count, x_hbm, taps_hbm, res_hbm, rate_hbm, skip_hbm, yb, sb, modes, decays,
    xb, xf, taps, res, rate, skip, ub, edges, states, gate_tail,
    outbox1, outbox2, outbox3, inbox1, inbox2, inbox3, ends, near, far, impulse,
    load_sems, x_sems, send1, recv1, send2, recv2, send3, recv3,
):
    me = lax.axis_index("ctx")
    tiles, rows = xf.shape[1:3]
    order = rate.shape[0]
    steps = rows // SUBS

    barrier = pltpu.get_barrier_semaphore()
    for d in range(1, count):
        @pl.when(me >= d)
        def _():
            pl.semaphore_signal(
                barrier, inc=1, device_id={"ctx": lax.rem(me - d + count, count)},
                device_id_type=MESH,
            )

    loads = [
        pltpu.make_async_copy(source, target, load_sems.at[i])
        for i, (source, target) in enumerate(
            [(rate_hbm, rate), (res_hbm, res), (taps_hbm, taps), (skip_hbm, skip)]
        )
    ]
    streams = [
        [
            pltpu.make_async_copy(
                x_hbm.at[p, :, pl.ds(tile * LANES, LANES)], xb.at[p, tile], x_sems.at[p, tile]
            )
            for p in range(3)
        ]
        for tile in range(tiles)
    ]
    loads[0].start()
    for p in (1, 2, 0):
        for tile in range(tiles):
            streams[tile][p].start()
    for load in loads[1:]:
        load.start()

    for d in range(1, count):
        @pl.when(me < d)
        def _():
            inbox1[d - 1] = jnp.zeros(inbox1.shape[1:], inbox1.dtype)
            inbox2[d - 1] = jnp.zeros(inbox2.shape[1:], inbox2.dtype)

    @pl.when(me == 0)
    def _():
        inbox3[...] = jnp.zeros_like(inbox3)

    gate_tail[...] = jnp.zeros_like(gate_tail)
    sub = lax.broadcasted_iota(jnp.int32, (SUBS, LANES), 0)
    distance = (sub * steps).astype(jnp.float32)
    remaining = ((SUBS - 1 - sub) * steps).astype(jnp.float32)

    def spread(table, r, tile, height=SUBS):
        return jnp.broadcast_to(
            table[r : r + 1, tile * LANES : (tile + 1) * LANES], (height, LANES)
        )

    loads[0].wait()
    mode_rate = rate[...]
    decay = jnp.exp(-mode_rate)
    decays[...] = decay
    for tile in range(tiles):
        for r in range(order):
            near[tile, r] = jnp.exp(-spread(mode_rate, r, tile) * remaining)
    for load in loads[1:]:
        load.wait()

    def send(out, box, d, send_sem, recv_sem):
        return pltpu.make_async_remote_copy(
            src_ref=out, dst_ref=box, send_sem=send_sem, recv_sem=recv_sem,
            device_id={"ctx": lax.rem(me + d, count)}, device_id_type=MESH,
        )

    ahead = range(count - 1, 0, -1)
    packets1 = {d: send(outbox1, inbox1.at[d - 1], d, send1.at[d - 1], recv1.at[d - 1]) for d in ahead}
    packets2 = {d: send(outbox2, inbox2.at[d - 1], d, send2.at[d - 1], recv2.at[d - 1]) for d in ahead}
    packet3 = send(outbox3, inbox3, 1, send3, recv3)

    def greet_and_send():
        @pl.when(me < count - 1)
        def _():
            pl.semaphore_wait(barrier, count - 1 - me)

        for d in ahead:
            @pl.when(me + d < count)
            def _():
                packets1[d].start()

        @pl.when(me < count - 1)
        def _():
            packet3.start()

    def previous(p, tile, k):
        last = xf[p, tile, pl.ds(k, SUBS, stride=steps), :]
        return jnp.where(sub == 0, 0.0, pltpu.roll(last, 1, 0))

    def tap_rows(p, tile):
        ln = pl.ds(tile * LANES, LANES)
        return [jnp.broadcast_to(taps[p, l : l + 1, ln], (SUBS, LANES)) for l in range(3)]

    for tile in range(tiles):
        for p in (1, 2):
            streams[tile][p].wait()
            first = tile * 8 + (p - 1) * 4
            edges[first : first + 2, :] = xb[p, tile, rows - 16 : rows, :].astype(jnp.float32)[14:16]
            edges[first + 2 : first + 4, :] = xb[p, tile, 0:16, :].astype(jnp.float32)[0:2]

    for tile in range(tiles):
        for p in (1, 2):
            xf[p, tile] = xb[p, tile].astype(jnp.float32)
        weight = {p: tap_rows(p, tile) for p in (1, 2)}
        a = [spread(decay, r, tile) for r in range(order)]

        def gate(k, carry):
            prev1, prev2, h = carry
            now = [xf[p, tile, pl.ds(k, SUBS, stride=steps), :] for p in (1, 2)]
            s = [
                weight[p][0] * now[p - 1] + weight[p][1] * prev1[p - 1] + weight[p][2] * prev2[p - 1]
                for p in (1, 2)
            ]
            u = jnp.where((sub == 0) & (k < 2), 0.0, s[0] * s[1])
            ub[tile, k] = u
            return now, prev1, [a[r] * h[r] + u for r in range(order)]

        start = (
            [previous(p, tile, steps - 1) for p in (1, 2)],
            [previous(p, tile, steps - 2) for p in (1, 2)],
            [jnp.zeros((SUBS, LANES), jnp.float32)] * order,
        )
        _, _, h = lax.fori_loop(0, steps, gate, start, unroll=8)
        for r in range(order):
            ends[tile, r] = h[r]
            states[tile, r : r + 1, :] = jnp.sum(near[tile, r] * h[r], axis=0, keepdims=True)
        if tile == 0:
            outbox1[:order] = states[0].astype(outbox1.dtype)
            outbox1[order:] = edges[...].astype(outbox1.dtype)
            for t in range(tiles):
                streams[t][0].wait()
                last = xb[0, t, rows - 16 : rows, :].astype(jnp.float32)
                gate_tail[2 * t : 2 * t + 2, :] = last[14:16]
            outbox3[...] = gate_tail[...].astype(outbox3.dtype)

            @pl.when(me > 0)
            def _():
                greet_and_send()

    outbox2[...] = states[1:].astype(outbox2.dtype)

    @pl.when(me == 0)
    def _():
        greet_and_send()

    for d in ahead:
        @pl.when(me + d < count)
        def _():
            packets2[d].start()

    grow = jnp.exp(mode_rate)
    hyper = jnp.tanh(mode_rate)
    gain = res[...] * jnp.sqrt(2.0 * hyper / (1.0 + hyper))
    span1 = jnp.exp(-steps * mode_rate)
    span2 = span1 * span1
    span4 = span2 * span2
    block_decay = span4 * span4
    overlap = jnp.sum(gain * grow, axis=0, keepdims=True)

    for tile in range(tiles):
        ln = pl.ds(tile * LANES, LANES)
        xf[0, tile] = xb[0, tile].astype(jnp.float32)
        w0, w1, w2 = tap_rows(0, tile)
        prev1, prev2 = previous(0, tile, steps - 1), previous(0, tile, steps - 2)
        for k in range(steps):
            now = xf[0, tile, pl.ds(k, SUBS, stride=steps), :]
            sb[tile, k] = w0 * now + w1 * prev1 + w2 * prev2
            prev1, prev2 = now, prev1

        time = lax.broadcasted_iota(jnp.int32, (steps, LANES), 0).astype(jnp.float32)
        response = add_up([
            spread(gain, r, tile, steps) * jnp.exp(-spread(mode_rate, r, tile, steps) * time)
            for r in range(order)
        ])
        impulse[tile] = response
        impulse[tile, 0:1, :] = response[0:1, :] + skip[0:1, ln]
        for first in range(0, steps, SUBS):
            total = [None] * SUBS
            for lag in range(0, first + 1, SUBS):
                source = first - lag
                u = [ub[tile, source + i] for i in range(SUBS)]
                for delay in range(max(0, lag - SUBS + 1), lag + SUBS):
                    tap = jnp.broadcast_to(impulse[tile, delay : delay + 1, :], (SUBS, LANES))
                    for i in range(SUBS):
                        k = source + i + delay - first
                        if 0 <= k < SUBS:
                            term = tap * u[i]
                            total[k] = term if total[k] is None else total[k] + term
            for k in range(SUBS):
                yb[tile, first + k] = total[k]
        for r in range(order):
            g = spread(gain, r, tile)
            far[tile, r] = g * jnp.exp(-spread(mode_rate, r, tile) * distance)
            total = ends[tile, r]
            for shift, table in ((1, span1), (2, span2), (4, span4)):
                total = total + jnp.where(
                    sub >= shift, spread(table, r, tile) * pltpu.roll(total, shift, 0), 0.0
                )
            ends[tile, r] = g * jnp.where(sub >= 1, pltpu.roll(total, 1, 0), 0.0)

    for d in range(1, count):
        @pl.when(me >= d)
        def _():
            packets1[d].wait_recv()

    heads = {}
    for tile in range(tiles):
        ln = pl.ds(tile * LANES, LANES)
        weight = [jnp.where(sub < 4, one, two) for one, two in zip(tap_rows(1, tile), tap_rows(2, tile))]

        def gated_head(mine, earlier):
            joined = jnp.where(sub % 4 >= 2, mine, earlier)
            s = (
                weight[0] * joined
                + weight[1] * pltpu.roll(joined, 1, 0)
                + weight[2] * pltpu.roll(joined, 2, 0)
            )
            u = s * pltpu.roll(s, 4, 0)
            return u[2:3], u[3:4]

        def edge_rows(d):
            if d == 0:
                return edges[8 * tile : 8 * tile + 8, :]
            if d == count:
                return jnp.zeros((8, LANES), jnp.float32)
            return inbox1[d - 1, order:, :].astype(jnp.float32)[8 * tile : 8 * tile + 8]

        heads[tile] = [gated_head(edge_rows(d), edge_rows(d + 1)) for d in range(count)]

    for tile in range(tiles):
        ln = pl.ds(tile * LANES, LANES)
        cut = slice(tile * LANES, (tile + 1) * LANES)
        if tile == 1:
            for d in range(1, count):
                @pl.when(me >= d)
                def _():
                    packets2[d].wait_recv()

        grown, kept = grow[:, cut], block_decay[:, cut]
        carried = jnp.zeros((order, LANES), jnp.float32)
        for d in range(count - 1, 0, -1):
            u0, u1 = heads[tile][d]
            arrived = inbox1[d - 1, :order, :] if tile == 0 else inbox2[d - 1, tile - 1]
            carried = kept * (carried + grown * (u0 + grown * u1)) + arrived.astype(jnp.float32)
        u0, u1 = heads[tile][0]
        entry = carried + grown * (u0 + grown * u1)
        for r in range(order):
            modes[tile, r] = ends[tile, r] + far[tile, r] * jnp.broadcast_to(
                entry[r : r + 1, :], (SUBS, LANES)
            )
        direct = skip[0:1, ln]
        yb[tile, 0, 0:1, :] = yb[tile, 0, 0:1, :] + direct * u0 - overlap[:, cut] * u1
        yb[tile, 1, 0:1, :] = yb[tile, 1, 0:1, :] + direct * u1

    @pl.when(me > 0)
    def _():
        packet3.wait_recv()

    tails = inbox3[...].astype(jnp.float32)
    for tile in range(tiles):
        ln = pl.ds(tile * LANES, LANES)
        w1, w2 = taps[0, 1:2, ln], taps[0, 2:3, ln]
        t2, t1 = tails[2 * tile : 2 * tile + 1], tails[2 * tile + 1 : 2 * tile + 2]
        sb[tile, 0, 0:1, :] = sb[tile, 0, 0:1, :] + w1 * t1 + w2 * t2
        sb[tile, 1, 0:1, :] = sb[tile, 1, 0:1, :] + w2 * t1

    for d in ahead:
        @pl.when(me + d < count)
        def _():
            packets1[d].wait_send()
            packets2[d].wait_send()

    @pl.when(me < count - 1)
    def _():
        packet3.wait_send()


def finish(yb, sb, modes, decays, out_hbm, of, ob, sems):
    tiles, steps = yb.shape[:2]
    order = modes.shape[1]
    stores = []
    for tile in range(tiles):
        ln = pl.ds(tile * LANES, LANES)
        a = [jnp.broadcast_to(decays[r : r + 1, ln], (SUBS, LANES)) for r in range(order)]

        def step(k, e):
            e = [a[r] * e[r] for r in range(order)]
            of[tile, pl.ds(k, SUBS, stride=steps), :] = sb[tile, k] * (yb[tile, k] + add_up(e))
            return e

        lax.fori_loop(0, steps, step, [modes[tile, r] for r in range(order)], unroll=4)
        ob[tile] = of[tile].astype(ob.dtype)
        stores.append(pltpu.make_async_copy(ob.at[tile], out_hbm.at[:, ln], sems.at[tile]))
        stores[tile].start()
    for store in stores:
        store.wait()


def body(hyena_in, short_taps, filter_residue, filter_rate, hyena_skip):
    count = lax.axis_size("ctx")
    _, rows, channels = hyena_in.shape
    order = filter_rate.shape[1]
    steps, tiles = rows // SUBS, channels // LANES
    f32, bf16 = jnp.float32, jnp.bfloat16
    signal = jax.ShapeDtypeStruct((tiles, steps, SUBS, LANES), f32)
    states = jax.ShapeDtypeStruct((tiles, order, SUBS, LANES), f32)
    table = jax.ShapeDtypeStruct((order, channels), f32)
    vmem = pl.BlockSpec(memory_space=pltpu.VMEM)
    packet = order + 8 * tiles
    per_mode = pltpu.VMEM((tiles, order, SUBS, LANES), f32)
    per_peer = pltpu.SemaphoreType.DMA((count - 1,))
    parts = pl.pallas_call(
        functools.partial(exchange, count),
        out_shape=[signal, signal, states, table],
        in_specs=[pl.BlockSpec(memory_space=pltpu.HBM)] * 5,
        out_specs=[vmem] * 4,
        scratch_shapes=[
            pltpu.VMEM((3, tiles, rows, LANES), bf16),
            pltpu.VMEM((3, tiles, rows, LANES), f32),
            pltpu.VMEM((3, 3, channels), f32),
            pltpu.VMEM((order, channels), f32),
            pltpu.VMEM((order, channels), f32),
            pltpu.VMEM((1, channels), f32),
            pltpu.VMEM((tiles, steps, SUBS, LANES), f32),
            pltpu.VMEM((8 * tiles, LANES), f32),
            pltpu.VMEM((tiles, order, LANES), f32),
            pltpu.VMEM((16, LANES), f32),
            pltpu.VMEM((packet, LANES), bf16),
            pltpu.VMEM((tiles - 1, order, LANES), bf16),
            pltpu.VMEM((16, LANES), bf16),
            pltpu.VMEM((count - 1, packet, LANES), bf16),
            pltpu.VMEM((count - 1, tiles - 1, order, LANES), bf16),
            pltpu.VMEM((16, LANES), bf16),
            per_mode,
            per_mode,
            per_mode,
            pltpu.VMEM((tiles, steps, LANES), f32),
            pltpu.SemaphoreType.DMA((4,)),
            pltpu.SemaphoreType.DMA((3, tiles)),
            per_peer,
            per_peer,
            per_peer,
            per_peer,
            pltpu.SemaphoreType.DMA,
            pltpu.SemaphoreType.DMA,
        ],
        compiler_params=pltpu.CompilerParams(
            collective_id=0, has_side_effects=True, vmem_limit_bytes=8 << 20
        ),
    )(*(
        pltpu.with_memory_space_constraint(value, pltpu.HBM)
        for value in (
            hyena_in, short_taps, filter_residue.T, filter_rate.T, hyena_skip.reshape(1, channels)
        )
    ))
    return pl.pallas_call(
        finish,
        out_shape=jax.ShapeDtypeStruct((rows, channels), bf16),
        in_specs=[vmem] * 4,
        out_specs=pl.BlockSpec(memory_space=pltpu.HBM),
        scratch_shapes=[
            pltpu.VMEM((tiles, rows, LANES), f32),
            pltpu.VMEM((tiles, rows, LANES), bf16),
            pltpu.SemaphoreType.DMA((tiles,)),
        ],
        compiler_params=pltpu.CompilerParams(vmem_limit_bytes=8 << 20),
    )(*parts)


def solution(mesh):
    return jax.shard_map(
        body,
        mesh=mesh,
        in_specs=(P(None, "ctx", "mp"), P(None, None, "mp"), P("mp", None), P("mp", None), P("mp")),
        out_specs=P("ctx", "mp"),
        check_vma=False,
    )
```

```python
import functools

import jax
import jax.numpy as jnp
from jax import lax
from jax.experimental import pallas as pl
from jax.experimental.pallas import tpu as pltpu
from jax.sharding import PartitionSpec as P

MESH = pl.DeviceIdType.MESH
SUBS = 8
LANES = 128


def add_up(terms):
    while len(terms) > 1:
        pairs = [terms[i] + terms[i + 1] for i in range(0, len(terms) - 1, 2)]
        terms = pairs + terms[2 * len(pairs) :]
    return terms[0]


def exchange(
    count, x_hbm, taps_hbm, res_hbm, rate_hbm, skip_hbm, ob,
    yb, sb, of, xb, xf, taps, res, rate, skip, ub, edges, states, gate_tail,
    outbox1, outbox2, outbox3, inbox1, inbox2, inbox3, ends, near, far, impulse,
    load_sems, x_sems, send1, recv1, send2, recv2, send3, recv3,
):
    me = lax.axis_index("ctx")
    tiles, rows = xf.shape[1:3]
    order = rate.shape[0]
    steps = rows // SUBS

    barrier = pltpu.get_barrier_semaphore()
    for d in range(1, count):
        @pl.when(me >= d)
        def _():
            pl.semaphore_signal(
                barrier, inc=1, device_id={"ctx": lax.rem(me - d + count, count)},
                device_id_type=MESH,
            )

    loads = [
        pltpu.make_async_copy(source, target, load_sems.at[i])
        for i, (source, target) in enumerate(
            [(rate_hbm, rate), (res_hbm, res), (taps_hbm, taps), (skip_hbm, skip)]
        )
    ]
    streams = [
        [
            pltpu.make_async_copy(
                x_hbm.at[p, :, pl.ds(tile * LANES, LANES)], xb.at[p, tile], x_sems.at[p, tile]
            )
            for p in range(3)
        ]
        for tile in range(tiles)
    ]
    loads[0].start()
    for p in (1, 2, 0):
        for tile in range(tiles):
            streams[tile][p].start()
    for load in loads[1:]:
        load.start()

    for d in range(1, count):
        @pl.when(me < d)
        def _():
            inbox1[d - 1] = jnp.zeros(inbox1.shape[1:], inbox1.dtype)
            inbox2[d - 1] = jnp.zeros(inbox2.shape[1:], inbox2.dtype)

    @pl.when(me == 0)
    def _():
        inbox3[...] = jnp.zeros_like(inbox3)

    gate_tail[...] = jnp.zeros_like(gate_tail)
    sub = lax.broadcasted_iota(jnp.int32, (SUBS, LANES), 0)
    distance = (sub * steps).astype(jnp.float32)
    remaining = ((SUBS - 1 - sub) * steps).astype(jnp.float32)

    def spread(table, r, tile, height=SUBS):
        return jnp.broadcast_to(
            table[r : r + 1, tile * LANES : (tile + 1) * LANES], (height, LANES)
        )

    loads[0].wait()
    mode_rate = rate[...]
    decay = jnp.exp(-mode_rate)
    for tile in range(tiles):
        for r in range(order):
            near[tile, r] = jnp.exp(-spread(mode_rate, r, tile) * remaining)
    for load in loads[1:]:
        load.wait()

    def send(out, box, d, send_sem, recv_sem):
        return pltpu.make_async_remote_copy(
            src_ref=out, dst_ref=box, send_sem=send_sem, recv_sem=recv_sem,
            device_id={"ctx": lax.rem(me + d, count)}, device_id_type=MESH,
        )

    ahead = range(count - 1, 0, -1)
    packets1 = {d: send(outbox1, inbox1.at[d - 1], d, send1.at[d - 1], recv1.at[d - 1]) for d in ahead}
    packets2 = {d: send(outbox2, inbox2.at[d - 1], d, send2.at[d - 1], recv2.at[d - 1]) for d in ahead}
    packet3 = send(outbox3, inbox3, 1, send3, recv3)

    def greet_and_send():
        @pl.when(me < count - 1)
        def _():
            pl.semaphore_wait(barrier, count - 1 - me)

        for d in ahead:
            @pl.when(me + d < count)
            def _():
                packets1[d].start()

        @pl.when(me < count - 1)
        def _():
            packet3.start()

    def previous(p, tile, k):
        last = xf[p, tile, pl.ds(k, SUBS, stride=steps), :]
        return jnp.where(sub == 0, 0.0, pltpu.roll(last, 1, 0))

    def tap_rows(p, tile):
        ln = pl.ds(tile * LANES, LANES)
        return [jnp.broadcast_to(taps[p, l : l + 1, ln], (SUBS, LANES)) for l in range(3)]

    for tile in range(tiles):
        for p in (1, 2):
            streams[tile][p].wait()
            first = tile * 8 + (p - 1) * 4
            edges[first : first + 2, :] = xb[p, tile, rows - 16 : rows, :].astype(jnp.float32)[14:16]
            edges[first + 2 : first + 4, :] = xb[p, tile, 0:16, :].astype(jnp.float32)[0:2]

    for tile in range(tiles):
        for p in (1, 2):
            xf[p, tile] = xb[p, tile].astype(jnp.float32)
        weight = {p: tap_rows(p, tile) for p in (1, 2)}
        a = [spread(decay, r, tile) for r in range(order)]

        def gate(k, carry):
            prev1, prev2, h = carry
            now = [xf[p, tile, pl.ds(k, SUBS, stride=steps), :] for p in (1, 2)]
            s = [
                weight[p][0] * now[p - 1] + weight[p][1] * prev1[p - 1] + weight[p][2] * prev2[p - 1]
                for p in (1, 2)
            ]
            u = jnp.where((sub == 0) & (k < 2), 0.0, s[0] * s[1])
            ub[tile, k] = u
            return now, prev1, [a[r] * h[r] + u for r in range(order)]

        start = (
            [previous(p, tile, steps - 1) for p in (1, 2)],
            [previous(p, tile, steps - 2) for p in (1, 2)],
            [jnp.zeros((SUBS, LANES), jnp.float32)] * order,
        )
        _, _, h = lax.fori_loop(0, steps, gate, start, unroll=8)
        for r in range(order):
            ends[tile, r] = h[r]
            states[tile, r : r + 1, :] = jnp.sum(near[tile, r] * h[r], axis=0, keepdims=True)
        if tile == 0:
            outbox1[:order] = states[0].astype(outbox1.dtype)
            outbox1[order:] = edges[...].astype(outbox1.dtype)
            for t in range(tiles):
                streams[t][0].wait()
                last = xb[0, t, rows - 16 : rows, :].astype(jnp.float32)
                gate_tail[2 * t : 2 * t + 2, :] = last[14:16]
            outbox3[...] = gate_tail[...].astype(outbox3.dtype)

            @pl.when(me > 0)
            def _():
                greet_and_send()

    outbox2[...] = states[1:].astype(outbox2.dtype)

    @pl.when(me == 0)
    def _():
        greet_and_send()

    for d in ahead:
        @pl.when(me + d < count)
        def _():
            packets2[d].start()

    grow = jnp.exp(mode_rate)
    hyper = jnp.tanh(mode_rate)
    gain = res[...] * jnp.sqrt(2.0 * hyper / (1.0 + hyper))
    span1 = jnp.exp(-steps * mode_rate)
    span2 = span1 * span1
    span4 = span2 * span2
    block_decay = span4 * span4
    overlap = jnp.sum(gain * grow, axis=0, keepdims=True)

    for tile in range(tiles):
        ln = pl.ds(tile * LANES, LANES)
        xf[0, tile] = xb[0, tile].astype(jnp.float32)
        w0, w1, w2 = tap_rows(0, tile)
        prev1, prev2 = previous(0, tile, steps - 1), previous(0, tile, steps - 2)
        for k in range(steps):
            now = xf[0, tile, pl.ds(k, SUBS, stride=steps), :]
            sb[tile, k] = w0 * now + w1 * prev1 + w2 * prev2
            prev1, prev2 = now, prev1

        time = lax.broadcasted_iota(jnp.int32, (steps, LANES), 0).astype(jnp.float32)
        response = add_up([
            spread(gain, r, tile, steps) * jnp.exp(-spread(mode_rate, r, tile, steps) * time)
            for r in range(order)
        ])
        impulse[tile] = response
        impulse[tile, 0:1, :] = response[0:1, :] + skip[0:1, ln]
        for first in range(0, steps, SUBS):
            total = [None] * SUBS
            for lag in range(0, first + 1, SUBS):
                source = first - lag
                u = [ub[tile, source + i] for i in range(SUBS)]
                for delay in range(max(0, lag - SUBS + 1), lag + SUBS):
                    tap = jnp.broadcast_to(impulse[tile, delay : delay + 1, :], (SUBS, LANES))
                    for i in range(SUBS):
                        k = source + i + delay - first
                        if 0 <= k < SUBS:
                            term = tap * u[i]
                            total[k] = term if total[k] is None else total[k] + term
            for k in range(SUBS):
                yb[tile, first + k] = total[k]
        for r in range(order):
            g = spread(gain, r, tile)
            far[tile, r] = g * jnp.exp(-spread(mode_rate, r, tile) * distance)
            total = ends[tile, r]
            for shift, table in ((1, span1), (2, span2), (4, span4)):
                total = total + jnp.where(
                    sub >= shift, spread(table, r, tile) * pltpu.roll(total, shift, 0), 0.0
                )
            ends[tile, r] = g * jnp.where(sub >= 1, pltpu.roll(total, 1, 0), 0.0)

    for d in range(1, count):
        @pl.when(me >= d)
        def _():
            packets1[d].wait_recv()

    heads = {}
    for tile in range(tiles):
        ln = pl.ds(tile * LANES, LANES)
        weight = [jnp.where(sub < 4, one, two) for one, two in zip(tap_rows(1, tile), tap_rows(2, tile))]

        def gated_head(mine, earlier):
            joined = jnp.where(sub % 4 >= 2, mine, earlier)
            s = (
                weight[0] * joined
                + weight[1] * pltpu.roll(joined, 1, 0)
                + weight[2] * pltpu.roll(joined, 2, 0)
            )
            u = s * pltpu.roll(s, 4, 0)
            return u[2:3], u[3:4]

        def edge_rows(d):
            if d == 0:
                return edges[8 * tile : 8 * tile + 8, :]
            if d == count:
                return jnp.zeros((8, LANES), jnp.float32)
            return inbox1[d - 1, order:, :].astype(jnp.float32)[8 * tile : 8 * tile + 8]

        heads[tile] = [gated_head(edge_rows(d), edge_rows(d + 1)) for d in range(count)]

    @pl.when(me > 0)
    def _():
        packet3.wait_recv()

    tails = inbox3[...].astype(jnp.float32)
    for tile in range(tiles):
        ln = pl.ds(tile * LANES, LANES)
        w1, w2 = taps[0, 1:2, ln], taps[0, 2:3, ln]
        t2, t1 = tails[2 * tile : 2 * tile + 1], tails[2 * tile + 1 : 2 * tile + 2]
        sb[tile, 0, 0:1, :] = sb[tile, 0, 0:1, :] + w1 * t1 + w2 * t2
        sb[tile, 1, 0:1, :] = sb[tile, 1, 0:1, :] + w2 * t1

    for tile in range(tiles):
        ln = pl.ds(tile * LANES, LANES)
        cut = slice(tile * LANES, (tile + 1) * LANES)
        if tile == 1:
            for d in range(1, count):
                @pl.when(me >= d)
                def _():
                    packets2[d].wait_recv()

        grown, kept = grow[:, cut], block_decay[:, cut]
        carried = jnp.zeros((order, LANES), jnp.float32)
        for d in range(count - 1, 0, -1):
            u0, u1 = heads[tile][d]
            arrived = inbox1[d - 1, :order, :] if tile == 0 else inbox2[d - 1, tile - 1]
            carried = kept * (carried + grown * (u0 + grown * u1)) + arrived.astype(jnp.float32)
        u0, u1 = heads[tile][0]
        entry = carried + grown * (u0 + grown * u1)
        direct = skip[0:1, ln]
        yb[tile, 0, 0:1, :] = yb[tile, 0, 0:1, :] + direct * u0 - overlap[:, cut] * u1
        yb[tile, 1, 0:1, :] = yb[tile, 1, 0:1, :] + direct * u1

        a = [spread(decay, r, tile) for r in range(order)]
        modes = [
            ends[tile, r] + far[tile, r] * jnp.broadcast_to(entry[r : r + 1, :], (SUBS, LANES))
            for r in range(order)
        ]

        def finish(k, e):
            e = [a[r] * e[r] for r in range(order)]
            of[tile, pl.ds(k, SUBS, stride=steps), :] = sb[tile, k] * (yb[tile, k] + add_up(e))
            return e

        lax.fori_loop(0, steps, finish, modes, unroll=4)
        ob[tile] = of[tile].astype(ob.dtype)

    for d in ahead:
        @pl.when(me + d < count)
        def _():
            packets1[d].wait_send()
            packets2[d].wait_send()

    @pl.when(me < count - 1)
    def _():
        packet3.wait_send()


def deliver(ob, out_hbm, sems):
    stores = [
        pltpu.make_async_copy(ob.at[tile], out_hbm.at[:, pl.ds(tile * LANES, LANES)], sems.at[tile])
        for tile in range(ob.shape[0])
    ]
    for store in stores:
        store.start()
    for store in stores:
        store.wait()


def body(hyena_in, short_taps, filter_residue, filter_rate, hyena_skip):
    count = lax.axis_size("ctx")
    _, rows, channels = hyena_in.shape
    order = filter_rate.shape[1]
    steps, tiles = rows // SUBS, channels // LANES
    f32, bf16 = jnp.float32, jnp.bfloat16
    signal = pltpu.VMEM((tiles, steps, SUBS, LANES), f32)
    vmem = pl.BlockSpec(memory_space=pltpu.VMEM)
    packet = order + 8 * tiles
    per_mode = pltpu.VMEM((tiles, order, SUBS, LANES), f32)
    per_peer = pltpu.SemaphoreType.DMA((count - 1,))
    result = pl.pallas_call(
        functools.partial(exchange, count),
        out_shape=jax.ShapeDtypeStruct((tiles, rows, LANES), bf16),
        in_specs=[pl.BlockSpec(memory_space=pltpu.HBM)] * 5,
        out_specs=vmem,
        scratch_shapes=[
            signal,
            signal,
            pltpu.VMEM((tiles, rows, LANES), f32),
            pltpu.VMEM((3, tiles, rows, LANES), bf16),
            pltpu.VMEM((3, tiles, rows, LANES), f32),
            pltpu.VMEM((3, 3, channels), f32),
            pltpu.VMEM((order, channels), f32),
            pltpu.VMEM((order, channels), f32),
            pltpu.VMEM((1, channels), f32),
            signal,
            pltpu.VMEM((8 * tiles, LANES), f32),
            pltpu.VMEM((tiles, order, LANES), f32),
            pltpu.VMEM((16, LANES), f32),
            pltpu.VMEM((packet, LANES), bf16),
            pltpu.VMEM((tiles - 1, order, LANES), bf16),
            pltpu.VMEM((16, LANES), bf16),
            pltpu.VMEM((count - 1, packet, LANES), bf16),
            pltpu.VMEM((count - 1, tiles - 1, order, LANES), bf16),
            pltpu.VMEM((16, LANES), bf16),
            per_mode,
            per_mode,
            per_mode,
            pltpu.VMEM((tiles, steps, LANES), f32),
            pltpu.SemaphoreType.DMA((4,)),
            pltpu.SemaphoreType.DMA((3, tiles)),
            per_peer,
            per_peer,
            per_peer,
            per_peer,
            pltpu.SemaphoreType.DMA,
            pltpu.SemaphoreType.DMA,
        ],
        compiler_params=pltpu.CompilerParams(
            collective_id=0, has_side_effects=True, vmem_limit_bytes=8 << 20
        ),
    )(*(
        pltpu.with_memory_space_constraint(value, pltpu.HBM)
        for value in (
            hyena_in, short_taps, filter_residue.T, filter_rate.T, hyena_skip.reshape(1, channels)
        )
    ))
    return pl.pallas_call(
        deliver,
        out_shape=jax.ShapeDtypeStruct((rows, channels), bf16),
        in_specs=[vmem],
        out_specs=pl.BlockSpec(memory_space=pltpu.HBM),
        scratch_shapes=[pltpu.SemaphoreType.DMA((tiles,))],
        compiler_params=pltpu.CompilerParams(vmem_limit_bytes=1 << 20),
    )(result)


def solution(mesh):
    return jax.shard_map(
        body,
        mesh=mesh,
        in_specs=(P(None, "ctx", "mp"), P(None, None, "mp"), P("mp", None), P("mp", None), P("mp")),
        out_specs=P("ctx", "mp"),
        check_vma=False,
    )
```

```python
import functools

import jax
import jax.numpy as jnp
from jax import lax
from jax.experimental import pallas as pl
from jax.experimental.pallas import tpu as pltpu
from jax.sharding import PartitionSpec as P

MESH = pl.DeviceIdType.MESH
SUBS = 8
LANES = 128


def add_up(terms):
    while len(terms) > 1:
        pairs = [terms[i] + terms[i + 1] for i in range(0, len(terms) - 1, 2)]
        terms = pairs + terms[2 * len(pairs) :]
    return terms[0]


def exchange(
    count, x_hbm, taps_hbm, res_hbm, rate_hbm, skip_hbm, ob,
    yb, sb, of, xb, xf, taps, res, rate, skip, ub, edges, states, gate_tail,
    pair_out, pair_in, far_out, far_in, tail_out, tail_in, ends, near, far, impulse,
    load_sems, x_sems, pair_sems, far_send, far_recv, tail_sems,
):
    me = lax.axis_index("ctx")
    pairs = count // 2
    pair, odd = me // 2, lax.rem(me, 2)
    tiles, rows = xf.shape[1:3]
    order = rate.shape[0]
    steps = rows // SUBS
    edge_from = tiles * order

    barrier = pltpu.get_barrier_semaphore()
    for d in range(1, count):
        @pl.when((me >= d) & ((lax.rem(me + d, 2) == 1) | (d == 1)))
        def _():
            pl.semaphore_signal(
                barrier, inc=1, device_id={"ctx": lax.rem(me - d + count, count)},
                device_id_type=MESH,
            )

    loads = [
        pltpu.make_async_copy(source, target, load_sems.at[i])
        for i, (source, target) in enumerate(
            [(rate_hbm, rate), (res_hbm, res), (taps_hbm, taps), (skip_hbm, skip)]
        )
    ]
    streams = [
        [
            pltpu.make_async_copy(
                x_hbm.at[p, :, pl.ds(tile * LANES, LANES)], xb.at[p, tile], x_sems.at[p, tile]
            )
            for p in range(3)
        ]
        for tile in range(tiles)
    ]
    loads[0].start()
    for p in (1, 2, 0):
        for tile in range(tiles):
            streams[tile][p].start()
    for load in loads[1:]:
        load.start()

    for e in range(1, pairs):
        @pl.when(pair < e)
        def _():
            far_in[e - 1] = jnp.zeros(far_in.shape[1:], far_in.dtype)

    @pl.when(odd == 0)
    def _():
        pair_in[...] = jnp.zeros_like(pair_in)

    @pl.when(me == 0)
    def _():
        tail_in[...] = jnp.zeros_like(tail_in)

    gate_tail[...] = jnp.zeros_like(gate_tail)
    sub = lax.broadcasted_iota(jnp.int32, (SUBS, LANES), 0)
    distance = (sub * steps).astype(jnp.float32)
    remaining = ((SUBS - 1 - sub) * steps).astype(jnp.float32)

    def spread(table, r, tile, height=SUBS):
        return jnp.broadcast_to(
            table[r : r + 1, tile * LANES : (tile + 1) * LANES], (height, LANES)
        )

    loads[0].wait()
    mode_rate = rate[...]
    decay = jnp.exp(-mode_rate)
    for tile in range(tiles):
        for r in range(order):
            near[tile, r] = jnp.exp(-spread(mode_rate, r, tile) * remaining)
    for load in loads[1:]:
        load.wait()

    def send(out, box, target, send_sem, recv_sem):
        return pltpu.make_async_remote_copy(
            src_ref=out, dst_ref=box, send_sem=send_sem, recv_sem=recv_sem,
            device_id={"ctx": lax.rem(target, count)}, device_id_type=MESH,
        )

    to_pair = send(pair_out, pair_in, me + 1, pair_sems.at[0], pair_sems.at[1])
    to_next = send(tail_out, tail_in, me + 1, tail_sems.at[0], tail_sems.at[1])
    to_far = {
        (e, core): send(
            far_out, far_in.at[e - 1], 2 * (pair + e) + core,
            far_send.at[e - 1, core], far_recv.at[e - 1],
        )
        for e in range(pairs - 1, 0, -1)
        for core in range(2)
    }

    def previous(p, tile, k):
        last = xf[p, tile, pl.ds(k, SUBS, stride=steps), :]
        return jnp.where(sub == 0, 0.0, pltpu.roll(last, 1, 0))

    def tap_rows(p, tile):
        ln = pl.ds(tile * LANES, LANES)
        return [jnp.broadcast_to(taps[p, l : l + 1, ln], (SUBS, LANES)) for l in range(3)]

    for tile in range(tiles):
        for p in (1, 2):
            streams[tile][p].wait()
            first = tile * 8 + (p - 1) * 4
            edges[first : first + 2, :] = xb[p, tile, rows - 16 : rows, :].astype(jnp.float32)[14:16]
            edges[first + 2 : first + 4, :] = xb[p, tile, 0:16, :].astype(jnp.float32)[0:2]

    for tile in range(tiles):
        for p in (1, 2):
            xf[p, tile] = xb[p, tile].astype(jnp.float32)
        weight = {p: tap_rows(p, tile) for p in (1, 2)}
        a = [spread(decay, r, tile) for r in range(order)]

        def gate(k, carry):
            prev1, prev2, h = carry
            now = [xf[p, tile, pl.ds(k, SUBS, stride=steps), :] for p in (1, 2)]
            s = [
                weight[p][0] * now[p - 1] + weight[p][1] * prev1[p - 1] + weight[p][2] * prev2[p - 1]
                for p in (1, 2)
            ]
            u = jnp.where((sub == 0) & (k < 2), 0.0, s[0] * s[1])
            ub[tile, k] = u
            return now, prev1, [a[r] * h[r] + u for r in range(order)]

        start = (
            [previous(p, tile, steps - 1) for p in (1, 2)],
            [previous(p, tile, steps - 2) for p in (1, 2)],
            [jnp.zeros((SUBS, LANES), jnp.float32)] * order,
        )
        _, _, h = lax.fori_loop(0, steps, gate, start, unroll=8)
        for r in range(order):
            ends[tile, r] = h[r]
            states[tile, r : r + 1, :] = jnp.sum(near[tile, r] * h[r], axis=0, keepdims=True)

    for tile in range(tiles):
        streams[tile][0].wait()
        last = xb[0, tile, rows - 16 : rows, :].astype(jnp.float32)
        gate_tail[2 * tile : 2 * tile + 2, :] = last[14:16]
        pair_out[tile * order : (tile + 1) * order] = states[tile].astype(pair_out.dtype)
    pair_out[edge_from:] = edges[...].astype(pair_out.dtype)
    tail_out[...] = gate_tail[...].astype(tail_out.dtype)

    @pl.when(odd == 0)
    def _():
        pl.semaphore_wait(barrier, 1)
        to_pair.start()
        to_next.start()

    grow = jnp.exp(mode_rate)
    hyper = jnp.tanh(mode_rate)
    gain = res[...] * jnp.sqrt(2.0 * hyper / (1.0 + hyper))
    span1 = jnp.exp(-steps * mode_rate)
    span2 = span1 * span1
    span4 = span2 * span2
    block_decay = span4 * span4
    pair_decay = block_decay * block_decay
    overlap = jnp.sum(gain * grow, axis=0, keepdims=True)

    for tile in range(tiles):
        ln = pl.ds(tile * LANES, LANES)
        xf[0, tile] = xb[0, tile].astype(jnp.float32)
        w0, w1, w2 = tap_rows(0, tile)
        prev1, prev2 = previous(0, tile, steps - 1), previous(0, tile, steps - 2)
        for k in range(steps):
            now = xf[0, tile, pl.ds(k, SUBS, stride=steps), :]
            sb[tile, k] = w0 * now + w1 * prev1 + w2 * prev2
            prev1, prev2 = now, prev1

        time = lax.broadcasted_iota(jnp.int32, (steps, LANES), 0).astype(jnp.float32)
        response = add_up([
            spread(gain, r, tile, steps) * jnp.exp(-spread(mode_rate, r, tile, steps) * time)
            for r in range(order)
        ])
        impulse[tile] = response
        impulse[tile, 0:1, :] = response[0:1, :] + skip[0:1, ln]
        for r in range(order):
            far[tile, r] = spread(gain, r, tile) * jnp.exp(-spread(mode_rate, r, tile) * distance)

    def gated_head(tile, mine, earlier):
        one, two = tap_rows(1, tile), tap_rows(2, tile)
        weight = [jnp.where(sub < 4, one[l], two[l]) for l in range(3)]
        joined = jnp.where(sub % 4 >= 2, mine, earlier)
        s = (
            weight[0] * joined
            + weight[1] * pltpu.roll(joined, 1, 0)
            + weight[2] * pltpu.roll(joined, 2, 0)
        )
        u = s * pltpu.roll(s, 4, 0)
        return u[2:3], u[3:4]

    def state_rows(box, tile):
        return box[tile * order : (tile + 1) * order].astype(jnp.float32)

    def edge_rows(box, tile):
        return box[edge_from:].astype(jnp.float32)[8 * tile : 8 * tile + 8]

    def cut(table, tile):
        return table[:, tile * LANES : (tile + 1) * LANES]

    def enter(tile, carried, u0, u1):
        grown = cut(grow, tile)
        return carried + grown * (u0 + grown * u1)

    @pl.when(odd == 1)
    def _():
        to_pair.wait_recv()
        joined = []
        for tile in range(tiles):
            mine, earlier = edges[8 * tile : 8 * tile + 8, :], edge_rows(pair_in, tile)
            u0, u1 = gated_head(tile, mine, earlier)
            both = states[tile] + cut(block_decay, tile) * enter(
                tile, state_rows(pair_in, tile), u0, u1
            )
            far_out[tile * order : (tile + 1) * order] = both.astype(far_out.dtype)
            joined.append(jnp.where(sub % 4 >= 2, earlier, mine))
        far_out[edge_from:] = jnp.concatenate(joined, axis=0).astype(far_out.dtype)

        @pl.when(pair < pairs - 1)
        def _():
            pl.semaphore_wait(barrier, count - 1 - me)
            for e in range(pairs - 1, 0, -1):
                @pl.when(pair + e < pairs)
                def _():
                    for core in range(2):
                        to_far[e, core].start()
            to_next.start()

    for tile in range(tiles):
        for first in range(0, steps, SUBS):
            total = [None] * SUBS
            for lag in range(0, first + 1, SUBS):
                source = first - lag
                u = [ub[tile, source + i] for i in range(SUBS)]
                for delay in range(max(0, lag - SUBS + 1), lag + SUBS):
                    tap = jnp.broadcast_to(impulse[tile, delay : delay + 1, :], (SUBS, LANES))
                    for i in range(SUBS):
                        k = source + i + delay - first
                        if 0 <= k < SUBS:
                            term = tap * u[i]
                            total[k] = term if total[k] is None else total[k] + term
            for k in range(SUBS):
                yb[tile, first + k] = total[k]
        for r in range(order):
            g = spread(gain, r, tile)
            total = ends[tile, r]
            for shift, table in ((1, span1), (2, span2), (4, span4)):
                total = total + jnp.where(
                    sub >= shift, spread(table, r, tile) * pltpu.roll(total, shift, 0), 0.0
                )
            ends[tile, r] = g * jnp.where(sub >= 1, pltpu.roll(total, 1, 0), 0.0)

    @pl.when(me > 0)
    def _():
        to_next.wait_recv()

    tails = tail_in[...].astype(jnp.float32)
    for tile in range(tiles):
        ln = pl.ds(tile * LANES, LANES)
        w1, w2 = taps[0, 1:2, ln], taps[0, 2:3, ln]
        t2, t1 = tails[2 * tile : 2 * tile + 1], tails[2 * tile + 1 : 2 * tile + 2]
        sb[tile, 0, 0:1, :] = sb[tile, 0, 0:1, :] + w1 * t1 + w2 * t2
        sb[tile, 1, 0:1, :] = sb[tile, 1, 0:1, :] + w2 * t1

    for e in range(1, pairs):
        @pl.when(pair >= e)
        def _():
            to_far[e, 0].wait_recv()

    for tile in range(tiles):
        ln = pl.ds(tile * LANES, LANES)
        carried = jnp.zeros((order, LANES), jnp.float32)
        earlier = jnp.zeros((SUBS, LANES), jnp.float32)
        for e in range(pairs - 1, 0, -1):
            box = far_in.at[e - 1]
            there = edge_rows(box, tile)
            u0, u1 = gated_head(tile, there, earlier)
            carried = cut(pair_decay, tile) * enter(tile, carried, u0, u1) + state_rows(box, tile)
            earlier = there
        mine, first = edges[8 * tile : 8 * tile + 8, :], edge_rows(pair_in, tile)
        u0, u1 = gated_head(tile, jnp.where(odd == 1, first, mine), earlier)
        entry = enter(tile, carried, u0, u1)
        v0, v1 = gated_head(tile, mine, first)
        second = enter(
            tile, cut(block_decay, tile) * entry + state_rows(pair_in, tile), v0, v1
        )
        entry = jnp.where(odd == 1, second, entry)
        u0, u1 = jnp.where(odd == 1, v0, u0), jnp.where(odd == 1, v1, u1)
        direct = skip[0:1, ln]
        yb[tile, 0, 0:1, :] = yb[tile, 0, 0:1, :] + direct * u0 - cut(overlap, tile) * u1
        yb[tile, 1, 0:1, :] = yb[tile, 1, 0:1, :] + direct * u1

        a = [spread(decay, r, tile) for r in range(order)]
        modes = [
            ends[tile, r] + far[tile, r] * jnp.broadcast_to(entry[r : r + 1, :], (SUBS, LANES))
            for r in range(order)
        ]

        def finish(k, e):
            e = [a[r] * e[r] for r in range(order)]
            of[tile, pl.ds(k, SUBS, stride=steps), :] = sb[tile, k] * (yb[tile, k] + add_up(e))
            return e

        lax.fori_loop(0, steps, finish, modes, unroll=4)
        ob[tile] = of[tile].astype(ob.dtype)

    @pl.when(odd == 0)
    def _():
        to_pair.wait_send()

    @pl.when(odd == 1)
    def _():
        for e in range(1, pairs):
            @pl.when(pair + e < pairs)
            def _():
                for core in range(2):
                    to_far[e, core].wait_send()

    @pl.when(me < count - 1)
    def _():
        to_next.wait_send()


def deliver(ob, out_hbm, sems):
    stores = [
        pltpu.make_async_copy(ob.at[tile], out_hbm.at[:, pl.ds(tile * LANES, LANES)], sems.at[tile])
        for tile in range(ob.shape[0])
    ]
    for store in stores:
        store.start()
    for store in stores:
        store.wait()


def body(hyena_in, short_taps, filter_residue, filter_rate, hyena_skip):
    count = lax.axis_size("ctx")
    _, rows, channels = hyena_in.shape
    order = filter_rate.shape[1]
    steps, tiles = rows // SUBS, channels // LANES
    f32, bf16 = jnp.float32, jnp.bfloat16
    signal = pltpu.VMEM((tiles, steps, SUBS, LANES), f32)
    vmem = pl.BlockSpec(memory_space=pltpu.VMEM)
    packet = (order + 8) * tiles
    per_mode = pltpu.VMEM((tiles, order, SUBS, LANES), f32)
    result = pl.pallas_call(
        functools.partial(exchange, count),
        out_shape=jax.ShapeDtypeStruct((tiles, rows, LANES), bf16),
        in_specs=[pl.BlockSpec(memory_space=pltpu.HBM)] * 5,
        out_specs=vmem,
        scratch_shapes=[
            signal,
            signal,
            pltpu.VMEM((tiles, rows, LANES), f32),
            pltpu.VMEM((3, tiles, rows, LANES), bf16),
            pltpu.VMEM((3, tiles, rows, LANES), f32),
            pltpu.VMEM((3, 3, channels), f32),
            pltpu.VMEM((order, channels), f32),
            pltpu.VMEM((order, channels), f32),
            pltpu.VMEM((1, channels), f32),
            signal,
            pltpu.VMEM((8 * tiles, LANES), f32),
            pltpu.VMEM((tiles, order, LANES), f32),
            pltpu.VMEM((16, LANES), f32),
            pltpu.VMEM((packet, LANES), bf16),
            pltpu.VMEM((packet, LANES), bf16),
            pltpu.VMEM((packet, LANES), bf16),
            pltpu.VMEM((count // 2 - 1, packet, LANES), bf16),
            pltpu.VMEM((16, LANES), bf16),
            pltpu.VMEM((16, LANES), bf16),
            per_mode,
            per_mode,
            per_mode,
            pltpu.VMEM((tiles, steps, LANES), f32),
            pltpu.SemaphoreType.DMA((4,)),
            pltpu.SemaphoreType.DMA((3, tiles)),
            pltpu.SemaphoreType.DMA((2,)),
            pltpu.SemaphoreType.DMA((count // 2 - 1, 2)),
            pltpu.SemaphoreType.DMA((count // 2 - 1,)),
            pltpu.SemaphoreType.DMA((2,)),
        ],
        compiler_params=pltpu.CompilerParams(
            collective_id=0, has_side_effects=True, vmem_limit_bytes=8 << 20
        ),
    )(*(
        pltpu.with_memory_space_constraint(value, pltpu.HBM)
        for value in (
            hyena_in, short_taps, filter_residue.T, filter_rate.T, hyena_skip.reshape(1, channels)
        )
    ))
    return pl.pallas_call(
        deliver,
        out_shape=jax.ShapeDtypeStruct((rows, channels), bf16),
        in_specs=[vmem],
        out_specs=pl.BlockSpec(memory_space=pltpu.HBM),
        scratch_shapes=[pltpu.SemaphoreType.DMA((tiles,))],
        compiler_params=pltpu.CompilerParams(vmem_limit_bytes=1 << 20),
    )(result)


def solution(mesh):
    return jax.shard_map(
        body,
        mesh=mesh,
        in_specs=(P(None, "ctx", "mp"), P(None, None, "mp"), P("mp", None), P("mp", None), P("mp")),
        out_specs=P("ctx", "mp"),
        check_vma=False,
    )
```

```python
import functools

import jax
import jax.numpy as jnp
from jax import lax
from jax.experimental import pallas as pl
from jax.experimental.pallas import tpu as pltpu
from jax.sharding import PartitionSpec as P

MESH = pl.DeviceIdType.MESH
SUBS = 8
LANES = 128


def add_up(terms):
    while len(terms) > 1:
        pairs = [terms[i] + terms[i + 1] for i in range(0, len(terms) - 1, 2)]
        terms = pairs + terms[2 * len(pairs) :]
    return terms[0]


def exchange(
    count, x_hbm, taps_hbm, res_hbm, rate_hbm, skip_hbm, ob,
    yb, sb, of, xb, xf, taps, res, rate, skip, ub, edges, states, gate_tail,
    outbox, tail_out, inbox, tail_in, ends, near, far, impulse,
    load_sems, x_sems, send_sems, recv_sems, tail_sems,
):
    me = lax.axis_index("ctx")
    tiles, rows = xf.shape[1:3]
    order = rate.shape[0]
    steps = rows // SUBS
    edge_from = tiles * order
    reach = range(1, count - 1)

    def hears(d):
        return (me > d) | (me == 1) if d == 1 else me > d

    barrier = pltpu.get_barrier_semaphore()
    for d in range(1, count):
        @pl.when((me > d) | ((me == d) & (d == 1)))
        def _():
            pl.semaphore_signal(
                barrier, inc=1, device_id={"ctx": lax.rem(me - d + count, count)},
                device_id_type=MESH,
            )

    loads = [
        pltpu.make_async_copy(source, target, load_sems.at[i])
        for i, (source, target) in enumerate(
            [(rate_hbm, rate), (res_hbm, res), (taps_hbm, taps), (skip_hbm, skip)]
        )
    ]
    streams = [
        [
            pltpu.make_async_copy(
                x_hbm.at[p, :, pl.ds(tile * LANES, LANES)], xb.at[p, tile], x_sems.at[p, tile]
            )
            for p in range(3)
        ]
        for tile in range(tiles)
    ]
    loads[0].start()
    for p in (1, 2, 0):
        for tile in range(tiles):
            streams[tile][p].start()
    for load in loads[1:]:
        load.start()

    for d in reach:
        @pl.when(jnp.logical_not(hears(d)))
        def _():
            inbox[d - 1] = jnp.zeros(inbox.shape[1:], inbox.dtype)

    @pl.when(me == 0)
    def _():
        tail_in[...] = jnp.zeros_like(tail_in)

    gate_tail[...] = jnp.zeros_like(gate_tail)
    sub = lax.broadcasted_iota(jnp.int32, (SUBS, LANES), 0)
    distance = (sub * steps).astype(jnp.float32)
    remaining = ((SUBS - 1 - sub) * steps).astype(jnp.float32)

    def spread(table, r, tile, height=SUBS):
        return jnp.broadcast_to(
            table[r : r + 1, tile * LANES : (tile + 1) * LANES], (height, LANES)
        )

    loads[0].wait()
    mode_rate = rate[...]
    decay = jnp.exp(-mode_rate)
    for tile in range(tiles):
        for r in range(order):
            near[tile, r] = jnp.exp(-spread(mode_rate, r, tile) * remaining)
    for load in loads[1:]:
        load.wait()

    def send(out, box, d, send_sem, recv_sem):
        return pltpu.make_async_remote_copy(
            src_ref=out, dst_ref=box, send_sem=send_sem, recv_sem=recv_sem,
            device_id={"ctx": lax.rem(me + d, count)}, device_id_type=MESH,
        )

    packets = {
        d: send(outbox, inbox.at[d - 1], d, send_sems.at[d - 1], recv_sems.at[d - 1]) for d in reach
    }
    tail_packet = send(tail_out, tail_in, 1, tail_sems.at[0], tail_sems.at[1])

    def speaks(d):
        return me + d < count if d == 1 else (me > 0) & (me + d < count)

    def greet_and_send():
        expected = jnp.where(me == 0, 1, count - 1 - me)

        @pl.when(me < count - 1)
        def _():
            pl.semaphore_wait(barrier, expected)

        for d in reach:
            @pl.when(speaks(d))
            def _():
                packets[d].start()

        @pl.when(me < count - 1)
        def _():
            tail_packet.start()

    def previous(p, tile, k):
        last = xf[p, tile, pl.ds(k, SUBS, stride=steps), :]
        return jnp.where(sub == 0, 0.0, pltpu.roll(last, 1, 0))

    def tap_rows(p, tile):
        ln = pl.ds(tile * LANES, LANES)
        return [jnp.broadcast_to(taps[p, l : l + 1, ln], (SUBS, LANES)) for l in range(3)]

    for tile in range(tiles):
        for p in (1, 2):
            streams[tile][p].wait()
            first = tile * 8 + (p - 1) * 4
            edges[first : first + 2, :] = xb[p, tile, rows - 16 : rows, :].astype(jnp.float32)[14:16]
            edges[first + 2 : first + 4, :] = xb[p, tile, 0:16, :].astype(jnp.float32)[0:2]

    for tile in range(tiles):
        for p in (1, 2):
            xf[p, tile] = xb[p, tile].astype(jnp.float32)
        weight = {p: tap_rows(p, tile) for p in (1, 2)}
        a = [spread(decay, r, tile) for r in range(order)]

        def gate(k, carry):
            prev1, prev2, h = carry
            now = [xf[p, tile, pl.ds(k, SUBS, stride=steps), :] for p in (1, 2)]
            s = [
                weight[p][0] * now[p - 1] + weight[p][1] * prev1[p - 1] + weight[p][2] * prev2[p - 1]
                for p in (1, 2)
            ]
            u = jnp.where((sub == 0) & (k < 2), 0.0, s[0] * s[1])
            ub[tile, k] = u
            return now, prev1, [a[r] * h[r] + u for r in range(order)]

        start = (
            [previous(p, tile, steps - 1) for p in (1, 2)],
            [previous(p, tile, steps - 2) for p in (1, 2)],
            [jnp.zeros((SUBS, LANES), jnp.float32)] * order,
        )
        _, _, h = lax.fori_loop(0, steps, gate, start, unroll=8)
        for r in range(order):
            ends[tile, r] = h[r]
            states[tile, r : r + 1, :] = jnp.sum(near[tile, r] * h[r], axis=0, keepdims=True)

    for tile in range(tiles):
        streams[tile][0].wait()
        last = xb[0, tile, rows - 16 : rows, :].astype(jnp.float32)
        gate_tail[2 * tile : 2 * tile + 2, :] = last[14:16]
        outbox[tile * order : (tile + 1) * order] = states[tile].astype(outbox.dtype)
    outbox[edge_from:] = edges[...].astype(outbox.dtype)
    tail_out[...] = gate_tail[...].astype(tail_out.dtype)

    @pl.when(me != 1)
    def _():
        greet_and_send()

    grow = jnp.exp(mode_rate)
    hyper = jnp.tanh(mode_rate)
    gain = res[...] * jnp.sqrt(2.0 * hyper / (1.0 + hyper))
    span1 = jnp.exp(-steps * mode_rate)
    span2 = span1 * span1
    span4 = span2 * span2
    block_decay = span4 * span4
    overlap = jnp.sum(gain * grow, axis=0, keepdims=True)

    for tile in range(tiles):
        ln = pl.ds(tile * LANES, LANES)
        xf[0, tile] = xb[0, tile].astype(jnp.float32)
        w0, w1, w2 = tap_rows(0, tile)
        prev1, prev2 = previous(0, tile, steps - 1), previous(0, tile, steps - 2)
        for k in range(steps):
            now = xf[0, tile, pl.ds(k, SUBS, stride=steps), :]
            sb[tile, k] = w0 * now + w1 * prev1 + w2 * prev2
            prev1, prev2 = now, prev1

        time = lax.broadcasted_iota(jnp.int32, (steps, LANES), 0).astype(jnp.float32)
        response = add_up([
            spread(gain, r, tile, steps) * jnp.exp(-spread(mode_rate, r, tile, steps) * time)
            for r in range(order)
        ])
        impulse[tile] = response
        impulse[tile, 0:1, :] = response[0:1, :] + skip[0:1, ln]
        for r in range(order):
            far[tile, r] = spread(gain, r, tile) * jnp.exp(-spread(mode_rate, r, tile) * distance)

    def gated_head(tile, mine, earlier):
        one, two = tap_rows(1, tile), tap_rows(2, tile)
        weight = [jnp.where(sub < 4, one[l], two[l]) for l in range(3)]
        joined = jnp.where(sub % 4 >= 2, mine, earlier)
        s = (
            weight[0] * joined
            + weight[1] * pltpu.roll(joined, 1, 0)
            + weight[2] * pltpu.roll(joined, 2, 0)
        )
        u = s * pltpu.roll(s, 4, 0)
        return u[2:3], u[3:4]

    def edge_rows(d, tile):
        if d == 0:
            return edges[8 * tile : 8 * tile + 8, :]
        if d not in reach:
            return jnp.zeros((8, LANES), jnp.float32)
        return inbox[d - 1, edge_from:, :].astype(jnp.float32)[8 * tile : 8 * tile + 8]

    def cut(table, tile):
        return table[:, tile * LANES : (tile + 1) * LANES]

    def enter(tile, carried, u0, u1):
        grown = cut(grow, tile)
        return carried + grown * (u0 + grown * u1)

    def after(tile, d, carried):
        u0, u1 = gated_head(tile, edge_rows(d, tile), edge_rows(d + 1, tile))
        end = states[tile] if d == 0 else inbox[d - 1, tile * order : (tile + 1) * order]
        return cut(block_decay, tile) * enter(tile, carried, u0, u1) + end.astype(jnp.float32)

    @pl.when(me == 1)
    def _():
        packets[1].wait_recv()
        for tile in range(tiles):
            both = after(tile, 0, after(tile, 1, jnp.zeros((order, LANES), jnp.float32)))
            outbox[tile * order : (tile + 1) * order] = both.astype(outbox.dtype)
        row = lax.broadcasted_iota(jnp.int32, (8 * tiles, LANES), 0)
        outbox[edge_from:] = jnp.where(row % 4 >= 2, 0.0, edges[...]).astype(outbox.dtype)
        greet_and_send()

    for tile in range(tiles):
        for first in range(0, steps, SUBS):
            total = [None] * SUBS
            for lag in range(0, first + 1, SUBS):
                source = first - lag
                u = [ub[tile, source + i] for i in range(SUBS)]
                for delay in range(max(0, lag - SUBS + 1), lag + SUBS):
                    tap = jnp.broadcast_to(impulse[tile, delay : delay + 1, :], (SUBS, LANES))
                    for i in range(SUBS):
                        k = source + i + delay - first
                        if 0 <= k < SUBS:
                            term = tap * u[i]
                            total[k] = term if total[k] is None else total[k] + term
            for k in range(SUBS):
                yb[tile, first + k] = total[k]
        for r in range(order):
            g = spread(gain, r, tile)
            total = ends[tile, r]
            for shift, table in ((1, span1), (2, span2), (4, span4)):
                total = total + jnp.where(
                    sub >= shift, spread(table, r, tile) * pltpu.roll(total, shift, 0), 0.0
                )
            ends[tile, r] = g * jnp.where(sub >= 1, pltpu.roll(total, 1, 0), 0.0)

    @pl.when(me > 0)
    def _():
        tail_packet.wait_recv()

    tails = tail_in[...].astype(jnp.float32)
    for tile in range(tiles):
        ln = pl.ds(tile * LANES, LANES)
        w1, w2 = taps[0, 1:2, ln], taps[0, 2:3, ln]
        t2, t1 = tails[2 * tile : 2 * tile + 1], tails[2 * tile + 1 : 2 * tile + 2]
        sb[tile, 0, 0:1, :] = sb[tile, 0, 0:1, :] + w1 * t1 + w2 * t2
        sb[tile, 1, 0:1, :] = sb[tile, 1, 0:1, :] + w2 * t1

    for d in reach:
        @pl.when(hears(d) & (me != 1))
        def _():
            packets[d].wait_recv()

    for tile in range(tiles):
        ln = pl.ds(tile * LANES, LANES)
        carried = jnp.zeros((order, LANES), jnp.float32)
        for d in reversed(reach):
            carried = after(tile, d, carried)
        u0, u1 = gated_head(tile, edge_rows(0, tile), edge_rows(1, tile))
        entry = enter(tile, carried, u0, u1)
        direct = skip[0:1, ln]
        yb[tile, 0, 0:1, :] = yb[tile, 0, 0:1, :] + direct * u0 - cut(overlap, tile) * u1
        yb[tile, 1, 0:1, :] = yb[tile, 1, 0:1, :] + direct * u1

        a = [spread(decay, r, tile) for r in range(order)]
        modes = [
            ends[tile, r] + far[tile, r] * jnp.broadcast_to(entry[r : r + 1, :], (SUBS, LANES))
            for r in range(order)
        ]

        def finish(k, e):
            e = [a[r] * e[r] for r in range(order)]
            of[tile, pl.ds(k, SUBS, stride=steps), :] = sb[tile, k] * (yb[tile, k] + add_up(e))
            return e

        lax.fori_loop(0, steps, finish, modes, unroll=4)
        ob[tile] = of[tile].astype(ob.dtype)

    for d in reach:
        @pl.when(speaks(d))
        def _():
            packets[d].wait_send()

    @pl.when(me < count - 1)
    def _():
        tail_packet.wait_send()


def deliver(ob, out_hbm, sems):
    stores = [
        pltpu.make_async_copy(ob.at[tile], out_hbm.at[:, pl.ds(tile * LANES, LANES)], sems.at[tile])
        for tile in range(ob.shape[0])
    ]
    for store in stores:
        store.start()
    for store in stores:
        store.wait()


def body(hyena_in, short_taps, filter_residue, filter_rate, hyena_skip):
    count = lax.axis_size("ctx")
    _, rows, channels = hyena_in.shape
    order = filter_rate.shape[1]
    steps, tiles = rows // SUBS, channels // LANES
    f32, bf16 = jnp.float32, jnp.bfloat16
    signal = pltpu.VMEM((tiles, steps, SUBS, LANES), f32)
    vmem = pl.BlockSpec(memory_space=pltpu.VMEM)
    packet = (order + 8) * tiles
    per_mode = pltpu.VMEM((tiles, order, SUBS, LANES), f32)
    result = pl.pallas_call(
        functools.partial(exchange, count),
        out_shape=jax.ShapeDtypeStruct((tiles, rows, LANES), bf16),
        in_specs=[pl.BlockSpec(memory_space=pltpu.HBM)] * 5,
        out_specs=vmem,
        scratch_shapes=[
            signal,
            signal,
            pltpu.VMEM((tiles, rows, LANES), f32),
            pltpu.VMEM((3, tiles, rows, LANES), bf16),
            pltpu.VMEM((3, tiles, rows, LANES), f32),
            pltpu.VMEM((3, 3, channels), f32),
            pltpu.VMEM((order, channels), f32),
            pltpu.VMEM((order, channels), f32),
            pltpu.VMEM((1, channels), f32),
            signal,
            pltpu.VMEM((8 * tiles, LANES), f32),
            pltpu.VMEM((tiles, order, LANES), f32),
            pltpu.VMEM((16, LANES), f32),
            pltpu.VMEM((packet, LANES), bf16),
            pltpu.VMEM((16, LANES), bf16),
            pltpu.VMEM((count - 2, packet, LANES), bf16),
            pltpu.VMEM((16, LANES), bf16),
            per_mode,
            per_mode,
            per_mode,
            pltpu.VMEM((tiles, steps, LANES), f32),
            pltpu.SemaphoreType.DMA((4,)),
            pltpu.SemaphoreType.DMA((3, tiles)),
            pltpu.SemaphoreType.DMA((count - 2,)),
            pltpu.SemaphoreType.DMA((count - 2,)),
            pltpu.SemaphoreType.DMA((2,)),
        ],
        compiler_params=pltpu.CompilerParams(
            collective_id=0, has_side_effects=True, vmem_limit_bytes=8 << 20
        ),
    )(*(
        pltpu.with_memory_space_constraint(value, pltpu.HBM)
        for value in (
            hyena_in, short_taps, filter_residue.T, filter_rate.T, hyena_skip.reshape(1, channels)
        )
    ))
    return pl.pallas_call(
        deliver,
        out_shape=jax.ShapeDtypeStruct((rows, channels), bf16),
        in_specs=[vmem],
        out_specs=pl.BlockSpec(memory_space=pltpu.HBM),
        scratch_shapes=[pltpu.SemaphoreType.DMA((tiles,))],
        compiler_params=pltpu.CompilerParams(vmem_limit_bytes=1 << 20),
    )(result)


def solution(mesh):
    return jax.shard_map(
        body,
        mesh=mesh,
        in_specs=(P(None, "ctx", "mp"), P(None, None, "mp"), P("mp", None), P("mp", None), P("mp")),
        out_specs=P("ctx", "mp"),
        check_vma=False,
    )
```

```python
import functools

import jax
import jax.numpy as jnp
from jax import lax
from jax.experimental import pallas as pl
from jax.experimental.pallas import tpu as pltpu
from jax.sharding import PartitionSpec as P

MESH = pl.DeviceIdType.MESH
SUBS = 8
LANES = 128


def add_up(terms):
    while len(terms) > 1:
        pairs = [terms[i] + terms[i + 1] for i in range(0, len(terms) - 1, 2)]
        terms = pairs + terms[2 * len(pairs) :]
    return terms[0]


def exchange(
    count, x_hbm, taps_hbm, res_hbm, rate_hbm, skip_hbm, ob,
    yb, sb, of, xb, xf, taps, res, rate, skip, ub, edges, states, gate_tail,
    outbox, tail_out, inbox, tail_in, ends, near, far, impulse,
    load_sems, x_sems, send_sems, recv_sems, tail_sems,
):
    me = lax.axis_index("ctx")
    tiles, rows = xf.shape[1:3]
    order = rate.shape[0]
    steps = rows // SUBS
    edge_from = tiles * order
    reach = range(1, count - 1)

    def hears(d):
        return (me > d) | (me == 1) if d == 1 else me > d

    barrier = pltpu.get_barrier_semaphore()
    for d in range(1, count):
        @pl.when((me > d) | ((me == d) & (d == 1)))
        def _():
            pl.semaphore_signal(
                barrier, inc=1, device_id={"ctx": lax.rem(me - d + count, count)},
                device_id_type=MESH,
            )

    loads = [
        pltpu.make_async_copy(source, target, load_sems.at[i])
        for i, (source, target) in enumerate(
            [(rate_hbm, rate), (res_hbm, res), (taps_hbm, taps), (skip_hbm, skip)]
        )
    ]
    streams = [
        [
            pltpu.make_async_copy(
                x_hbm.at[p, :, pl.ds(tile * LANES, LANES)], xb.at[p, tile], x_sems.at[p, tile]
            )
            for p in range(3)
        ]
        for tile in range(tiles)
    ]
    loads[0].start()
    for p in (1, 2, 0):
        for tile in range(tiles):
            streams[tile][p].start()
    for load in loads[1:]:
        load.start()

    for d in reach:
        @pl.when(jnp.logical_not(hears(d)))
        def _():
            inbox[d - 1] = jnp.zeros(inbox.shape[1:], inbox.dtype)

    @pl.when(me == 0)
    def _():
        tail_in[...] = jnp.zeros_like(tail_in)

    gate_tail[...] = jnp.zeros_like(gate_tail)
    sub = lax.broadcasted_iota(jnp.int32, (SUBS, LANES), 0)
    distance = (sub * steps).astype(jnp.float32)
    remaining = ((SUBS - 1 - sub) * steps).astype(jnp.float32)

    def spread(table, r, tile, height=SUBS):
        return jnp.broadcast_to(
            table[r : r + 1, tile * LANES : (tile + 1) * LANES], (height, LANES)
        )

    loads[0].wait()
    mode_rate = rate[...]
    decay = jnp.exp(-mode_rate)
    for tile in range(tiles):
        for r in range(order):
            near[tile, r] = jnp.exp(-spread(mode_rate, r, tile) * remaining)
    for load in loads[1:]:
        load.wait()

    def send(out, box, d, send_sem, recv_sem):
        return pltpu.make_async_remote_copy(
            src_ref=out, dst_ref=box, send_sem=send_sem, recv_sem=recv_sem,
            device_id={"ctx": lax.rem(me + d, count)}, device_id_type=MESH,
        )

    packets = {
        d: send(outbox, inbox.at[d - 1], d, send_sems.at[d - 1], recv_sems.at[d - 1]) for d in reach
    }
    tail_packet = send(tail_out, tail_in, 1, tail_sems.at[0], tail_sems.at[1])

    def speaks(d):
        return me + d < count if d == 1 else (me > 0) & (me + d < count)

    def greet_and_send():
        expected = jnp.where(me == 0, 1, count - 1 - me)

        @pl.when(me < count - 1)
        def _():
            pl.semaphore_wait(barrier, expected)

        for d in reach:
            @pl.when(speaks(d))
            def _():
                packets[d].start()

        @pl.when(me < count - 1)
        def _():
            tail_packet.start()

    def previous(p, tile, k):
        last = xf[p, tile, pl.ds(k, SUBS, stride=steps), :]
        return jnp.where(sub == 0, 0.0, pltpu.roll(last, 1, 0))

    def tap_rows(p, tile):
        ln = pl.ds(tile * LANES, LANES)
        return [jnp.broadcast_to(taps[p, l : l + 1, ln], (SUBS, LANES)) for l in range(3)]

    for tile in range(tiles):
        for p in (1, 2):
            streams[tile][p].wait()
            first = tile * 8 + (p - 1) * 4
            edges[first : first + 2, :] = xb[p, tile, rows - 16 : rows, :].astype(jnp.float32)[14:16]
            edges[first + 2 : first + 4, :] = xb[p, tile, 0:16, :].astype(jnp.float32)[0:2]

    for tile in range(tiles):
        for p in (1, 2):
            xf[p, tile] = xb[p, tile].astype(jnp.float32)
        weight = {p: tap_rows(p, tile) for p in (1, 2)}
        a = [spread(decay, r, tile) for r in range(order)]

        def gate(k, carry, opening=False):
            prev1, prev2, h = carry
            now = [xf[p, tile, pl.ds(k, SUBS, stride=steps), :] for p in (1, 2)]
            s = [
                weight[p][0] * now[p - 1] + weight[p][1] * prev1[p - 1] + weight[p][2] * prev2[p - 1]
                for p in (1, 2)
            ]
            u = s[0] * s[1]
            if opening:
                u = jnp.where(sub == 0, 0.0, u)
            ub[tile, k] = u
            return now, prev1, [a[r] * h[r] + u for r in range(order)]

        start = (
            [previous(p, tile, steps - 1) for p in (1, 2)],
            [previous(p, tile, steps - 2) for p in (1, 2)],
            [jnp.zeros((SUBS, LANES), jnp.float32)] * order,
        )
        start = gate(1, gate(0, start, True), True)
        _, _, h = lax.fori_loop(2, steps, gate, start, unroll=6)
        for r in range(order):
            ends[tile, r] = h[r]
            states[tile, r : r + 1, :] = jnp.sum(near[tile, r] * h[r], axis=0, keepdims=True)

    for tile in range(tiles):
        streams[tile][0].wait()
        last = xb[0, tile, rows - 16 : rows, :].astype(jnp.float32)
        gate_tail[2 * tile : 2 * tile + 2, :] = last[14:16]
        outbox[tile * order : (tile + 1) * order] = states[tile].astype(outbox.dtype)
    outbox[edge_from:] = edges[...].astype(outbox.dtype)
    tail_out[...] = gate_tail[...].astype(tail_out.dtype)

    @pl.when(me != 1)
    def _():
        greet_and_send()

    grow = jnp.exp(mode_rate)
    hyper = jnp.tanh(mode_rate)
    gain = res[...] * jnp.sqrt(2.0 * hyper / (1.0 + hyper))
    span1 = jnp.exp(-steps * mode_rate)
    span2 = span1 * span1
    span4 = span2 * span2
    block_decay = span4 * span4
    overlap = jnp.sum(gain * grow, axis=0, keepdims=True)

    for tile in range(tiles):
        ln = pl.ds(tile * LANES, LANES)
        xf[0, tile] = xb[0, tile].astype(jnp.float32)
        w0, w1, w2 = tap_rows(0, tile)
        prev1, prev2 = previous(0, tile, steps - 1), previous(0, tile, steps - 2)
        for k in range(steps):
            now = xf[0, tile, pl.ds(k, SUBS, stride=steps), :]
            sb[tile, k] = w0 * now + w1 * prev1 + w2 * prev2
            prev1, prev2 = now, prev1

        time = lax.broadcasted_iota(jnp.int32, (steps, LANES), 0).astype(jnp.float32)
        response = add_up([
            spread(gain, r, tile, steps) * jnp.exp(-spread(mode_rate, r, tile, steps) * time)
            for r in range(order)
        ])
        impulse[tile] = response
        impulse[tile, 0:1, :] = response[0:1, :] + skip[0:1, ln]
        for r in range(order):
            far[tile, r] = spread(gain, r, tile) * jnp.exp(-spread(mode_rate, r, tile) * distance)

    def gated_head(tile, mine, earlier):
        one, two = tap_rows(1, tile), tap_rows(2, tile)
        weight = [jnp.where(sub < 4, one[l], two[l]) for l in range(3)]
        joined = jnp.where(sub % 4 >= 2, mine, earlier)
        s = (
            weight[0] * joined
            + weight[1] * pltpu.roll(joined, 1, 0)
            + weight[2] * pltpu.roll(joined, 2, 0)
        )
        u = s * pltpu.roll(s, 4, 0)
        return u[2:3], u[3:4]

    def edge_rows(d, tile):
        if d == 0:
            return edges[8 * tile : 8 * tile + 8, :]
        if d not in reach:
            return jnp.zeros((8, LANES), jnp.float32)
        return inbox[d - 1, edge_from:, :].astype(jnp.float32)[8 * tile : 8 * tile + 8]

    def cut(table, tile):
        return table[:, tile * LANES : (tile + 1) * LANES]

    def enter(tile, carried, u0, u1):
        grown = cut(grow, tile)
        return carried + grown * (u0 + grown * u1)

    def after(tile, d, carried):
        u0, u1 = gated_head(tile, edge_rows(d, tile), edge_rows(d + 1, tile))
        end = states[tile] if d == 0 else inbox[d - 1, tile * order : (tile + 1) * order]
        return cut(block_decay, tile) * enter(tile, carried, u0, u1) + end.astype(jnp.float32)

    @pl.when(me == 1)
    def _():
        packets[1].wait_recv()
        for tile in range(tiles):
            both = after(tile, 0, after(tile, 1, jnp.zeros((order, LANES), jnp.float32)))
            outbox[tile * order : (tile + 1) * order] = both.astype(outbox.dtype)
        row = lax.broadcasted_iota(jnp.int32, (8 * tiles, LANES), 0)
        outbox[edge_from:] = jnp.where(row % 4 >= 2, 0.0, edges[...]).astype(outbox.dtype)
        greet_and_send()

    for tile in range(tiles):
        for first in range(0, steps, SUBS):
            total = [None] * SUBS
            for lag in range(0, first + 1, SUBS):
                source = first - lag
                u = [ub[tile, source + i] for i in range(SUBS)]
                for delay in range(max(0, lag - SUBS + 1), lag + SUBS):
                    tap = jnp.broadcast_to(impulse[tile, delay : delay + 1, :], (SUBS, LANES))
                    for i in range(SUBS):
                        k = source + i + delay - first
                        if 0 <= k < SUBS:
                            term = tap * u[i]
                            total[k] = term if total[k] is None else total[k] + term
            for k in range(SUBS):
                yb[tile, first + k] = total[k]
        for r in range(order):
            g = spread(gain, r, tile)
            total = ends[tile, r]
            for shift, table in ((1, span1), (2, span2), (4, span4)):
                total = total + jnp.where(
                    sub >= shift, spread(table, r, tile) * pltpu.roll(total, shift, 0), 0.0
                )
            ends[tile, r] = g * jnp.where(sub >= 1, pltpu.roll(total, 1, 0), 0.0)

    @pl.when(me > 0)
    def _():
        tail_packet.wait_recv()

    tails = tail_in[...].astype(jnp.float32)
    for tile in range(tiles):
        ln = pl.ds(tile * LANES, LANES)
        w1, w2 = taps[0, 1:2, ln], taps[0, 2:3, ln]
        t2, t1 = tails[2 * tile : 2 * tile + 1], tails[2 * tile + 1 : 2 * tile + 2]
        sb[tile, 0, 0:1, :] = sb[tile, 0, 0:1, :] + w1 * t1 + w2 * t2
        sb[tile, 1, 0:1, :] = sb[tile, 1, 0:1, :] + w2 * t1

    carried = [jnp.zeros((order, LANES), jnp.float32)] * tiles
    for d in reversed(reach):
        @pl.when(hears(d) & (me != 1))
        def _():
            packets[d].wait_recv()

        carried = [after(tile, d, carried[tile]) for tile in range(tiles)]

    for tile in range(tiles):
        ln = pl.ds(tile * LANES, LANES)
        u0, u1 = gated_head(tile, edge_rows(0, tile), edge_rows(1, tile))
        entry = enter(tile, carried[tile], u0, u1)
        direct = skip[0:1, ln]
        yb[tile, 0, 0:1, :] = yb[tile, 0, 0:1, :] + direct * u0 - cut(overlap, tile) * u1
        yb[tile, 1, 0:1, :] = yb[tile, 1, 0:1, :] + direct * u1

        a = [spread(decay, r, tile) for r in range(order)]
        modes = [
            ends[tile, r] + far[tile, r] * jnp.broadcast_to(entry[r : r + 1, :], (SUBS, LANES))
            for r in range(order)
        ]

        def finish(k, e):
            e = [a[r] * e[r] for r in range(order)]
            of[tile, pl.ds(k, SUBS, stride=steps), :] = sb[tile, k] * (yb[tile, k] + add_up(e))
            return e

        lax.fori_loop(0, steps, finish, modes, unroll=8)
        ob[tile] = of[tile].astype(ob.dtype)

    for d in reach:
        @pl.when(speaks(d))
        def _():
            packets[d].wait_send()

    @pl.when(me < count - 1)
    def _():
        tail_packet.wait_send()


def deliver(ob, out_hbm, sems):
    stores = [
        pltpu.make_async_copy(ob.at[tile], out_hbm.at[:, pl.ds(tile * LANES, LANES)], sems.at[tile])
        for tile in range(ob.shape[0])
    ]
    for store in stores:
        store.start()
    for store in stores:
        store.wait()


def body(hyena_in, short_taps, filter_residue, filter_rate, hyena_skip):
    count = lax.axis_size("ctx")
    _, rows, channels = hyena_in.shape
    order = filter_rate.shape[1]
    steps, tiles = rows // SUBS, channels // LANES
    f32, bf16 = jnp.float32, jnp.bfloat16
    signal = pltpu.VMEM((tiles, steps, SUBS, LANES), f32)
    vmem = pl.BlockSpec(memory_space=pltpu.VMEM)
    packet = (order + 8) * tiles
    per_mode = pltpu.VMEM((tiles, order, SUBS, LANES), f32)
    result = pl.pallas_call(
        functools.partial(exchange, count),
        out_shape=jax.ShapeDtypeStruct((tiles, rows, LANES), bf16),
        in_specs=[pl.BlockSpec(memory_space=pltpu.HBM)] * 5,
        out_specs=vmem,
        scratch_shapes=[
            signal,
            signal,
            pltpu.VMEM((tiles, rows, LANES), f32),
            pltpu.VMEM((3, tiles, rows, LANES), bf16),
            pltpu.VMEM((3, tiles, rows, LANES), f32),
            pltpu.VMEM((3, 3, channels), f32),
            pltpu.VMEM((order, channels), f32),
            pltpu.VMEM((order, channels), f32),
            pltpu.VMEM((1, channels), f32),
            signal,
            pltpu.VMEM((8 * tiles, LANES), f32),
            pltpu.VMEM((tiles, order, LANES), f32),
            pltpu.VMEM((16, LANES), f32),
            pltpu.VMEM((packet, LANES), bf16),
            pltpu.VMEM((16, LANES), bf16),
            pltpu.VMEM((count - 2, packet, LANES), bf16),
            pltpu.VMEM((16, LANES), bf16),
            per_mode,
            per_mode,
            per_mode,
            pltpu.VMEM((tiles, steps, LANES), f32),
            pltpu.SemaphoreType.DMA((4,)),
            pltpu.SemaphoreType.DMA((3, tiles)),
            pltpu.SemaphoreType.DMA((count - 2,)),
            pltpu.SemaphoreType.DMA((count - 2,)),
            pltpu.SemaphoreType.DMA((2,)),
        ],
        compiler_params=pltpu.CompilerParams(
            collective_id=0, has_side_effects=True, vmem_limit_bytes=8 << 20
        ),
    )(*(
        pltpu.with_memory_space_constraint(value, pltpu.HBM)
        for value in (
            hyena_in, short_taps, filter_residue.T, filter_rate.T, hyena_skip.reshape(1, channels)
        )
    ))
    return pl.pallas_call(
        deliver,
        out_shape=jax.ShapeDtypeStruct((rows, channels), bf16),
        in_specs=[vmem],
        out_specs=pl.BlockSpec(memory_space=pltpu.HBM),
        scratch_shapes=[pltpu.SemaphoreType.DMA((tiles,))],
        compiler_params=pltpu.CompilerParams(vmem_limit_bytes=1 << 20),
    )(result)


def solution(mesh):
    return jax.shard_map(
        body,
        mesh=mesh,
        in_specs=(P(None, "ctx", "mp"), P(None, None, "mp"), P("mp", None), P("mp", None), P("mp")),
        out_specs=P("ctx", "mp"),
        check_vma=False,
    )
```

```python
import functools

import jax
import jax.numpy as jnp
from jax import lax
from jax.experimental import pallas as pl
from jax.experimental.pallas import tpu as pltpu
from jax.sharding import PartitionSpec as P

MESH = pl.DeviceIdType.MESH
SUBS = 8
LANES = 128
CHUNKS = 4


def add_up(terms):
    while len(terms) > 1:
        pairs = [terms[i] + terms[i + 1] for i in range(0, len(terms) - 1, 2)]
        terms = pairs + terms[2 * len(pairs) :]
    return terms[0]


def exchange(
    count, x_hbm, taps_hbm, res_hbm, rate_hbm, skip_hbm, ob,
    yb, sb, of, xb, xf, taps, res, rate, skip, ub, edges, states, gate_tail,
    outbox, tail_out, inbox, tail_in, ends, near, far, impulse,
    load_sems, x_sems, send_sems, recv_sems, tail_sems,
):
    me = lax.axis_index("ctx")
    tiles, rows = xb.shape[1:3]
    order = rate.shape[0]
    steps = rows // SUBS
    edge_from = tiles * order
    reach = range(1, count - 1)

    def hears(d):
        return (me > d) | (me == 1) if d == 1 else me > d

    barrier = pltpu.get_barrier_semaphore()
    for d in range(1, count):
        @pl.when((me > d) | ((me == d) & (d == 1)))
        def _():
            pl.semaphore_signal(
                barrier, inc=1, device_id={"ctx": lax.rem(me - d + count, count)},
                device_id_type=MESH,
            )

    loads = [
        pltpu.make_async_copy(source, target, load_sems.at[i])
        for i, (source, target) in enumerate(
            [(rate_hbm, rate), (res_hbm, res), (taps_hbm, taps), (skip_hbm, skip)]
        )
    ]
    streams = [
        [
            pltpu.make_async_copy(
                x_hbm.at[p, :, pl.ds(tile * LANES, LANES)], xb.at[p, tile], x_sems.at[p, tile]
            )
            for p in range(3)
        ]
        for tile in range(tiles)
    ]
    loads[0].start()
    for p in (1, 2, 0):
        for tile in range(tiles):
            streams[tile][p].start()
    for load in loads[1:]:
        load.start()

    for d in reach:
        @pl.when(jnp.logical_not(hears(d)))
        def _():
            inbox[d - 1] = jnp.zeros(inbox.shape[1:], inbox.dtype)

    @pl.when(me == 0)
    def _():
        tail_in[...] = jnp.zeros_like(tail_in)

    gate_tail[...] = jnp.zeros_like(gate_tail)
    sub = lax.broadcasted_iota(jnp.int32, (SUBS, LANES), 0)
    distance = (sub * steps).astype(jnp.float32)
    remaining = ((SUBS - 1 - sub) * steps).astype(jnp.float32)

    def spread(table, r, tile, height=SUBS):
        return jnp.broadcast_to(
            table[r : r + 1, tile * LANES : (tile + 1) * LANES], (height, LANES)
        )

    loads[0].wait()
    mode_rate = rate[...]
    decay = jnp.exp(-mode_rate)
    for tile in range(tiles):
        for r in range(order):
            near[tile, r] = jnp.exp(-spread(mode_rate, r, tile) * remaining)
    for load in loads[1:]:
        load.wait()

    def send(out, box, d, send_sem, recv_sem):
        return pltpu.make_async_remote_copy(
            src_ref=out, dst_ref=box, send_sem=send_sem, recv_sem=recv_sem,
            device_id={"ctx": lax.rem(me + d, count)}, device_id_type=MESH,
        )

    packets = {
        d: send(outbox, inbox.at[d - 1], d, send_sems.at[d - 1], recv_sems.at[d - 1]) for d in reach
    }
    tail_packet = send(tail_out, tail_in, 1, tail_sems.at[0], tail_sems.at[1])

    def speaks(d):
        return me + d < count if d == 1 else (me > 0) & (me + d < count)

    def greet_and_send():
        expected = jnp.where(me == 0, 1, count - 1 - me)

        @pl.when(me < count - 1)
        def _():
            pl.semaphore_wait(barrier, expected)

        for d in reach:
            @pl.when(speaks(d))
            def _():
                packets[d].start()

    def previous(p, tile, k):
        last = xf[p, tile, pl.ds(k, SUBS, stride=steps), :]
        return jnp.where(sub == 0, 0.0, pltpu.roll(last, 1, 0))

    def tap_rows(p, tile):
        ln = pl.ds(tile * LANES, LANES)
        return [jnp.broadcast_to(taps[p, l : l + 1, ln], (SUBS, LANES)) for l in range(3)]

    for tile in range(tiles):
        for p in (1, 2):
            streams[tile][p].wait()
            first = tile * 8 + (p - 1) * 4
            edges[first : first + 2, :] = xb[p, tile, rows - 16 : rows, :].astype(jnp.float32)[14:16]
            edges[first + 2 : first + 4, :] = xb[p, tile, 0:16, :].astype(jnp.float32)[0:2]

    for tile in range(tiles):
        for p in (1, 2):
            xf[p, tile, :rows, :] = xb[p, tile].astype(jnp.float32)
        weight = {p: tap_rows(p, tile) for p in (1, 2)}
        a = [spread(decay, r, tile) for r in range(order)]

        def gate(k, carry, opening=False):
            prev1, prev2, h = carry
            now = [xf[p, tile, pl.ds(k, SUBS, stride=steps), :] for p in (1, 2)]
            s = [
                weight[p][0] * now[p - 1] + weight[p][1] * prev1[p - 1] + weight[p][2] * prev2[p - 1]
                for p in (1, 2)
            ]
            u = s[0] * s[1]
            if opening:
                u = jnp.where(sub == 0, 0.0, u)
            ub[tile, k] = u
            return now, prev1, [a[r] * h[r] + u for r in range(order)]

        start = (
            [previous(p, tile, steps - 1) for p in (1, 2)],
            [previous(p, tile, steps - 2) for p in (1, 2)],
            [jnp.zeros((SUBS, LANES), jnp.float32)] * order,
        )
        start = gate(1, gate(0, start, True), True)
        _, _, h = lax.fori_loop(2, steps, gate, start, unroll=6)
        for r in range(order):
            ends[tile, r] = h[r]
            states[tile, r : r + 1, :] = jnp.sum(near[tile, r] * h[r], axis=0, keepdims=True)

    for tile in range(tiles):
        outbox[tile * order : (tile + 1) * order] = states[tile].astype(outbox.dtype)
    outbox[edge_from:] = edges[...].astype(outbox.dtype)

    @pl.when(me != 1)
    def _():
        greet_and_send()

    for tile in range(tiles):
        streams[tile][0].wait()
        last = xb[0, tile, rows - 16 : rows, :].astype(jnp.float32)
        gate_tail[2 * tile : 2 * tile + 2, :] = last[14:16]
    tail_out[...] = gate_tail[...].astype(tail_out.dtype)

    @pl.when((me < count - 1) & (me != 1))
    def _():
        tail_packet.start()

    grow = jnp.exp(mode_rate)
    hyper = jnp.tanh(mode_rate)
    gain = res[...] * jnp.sqrt(2.0 * hyper / (1.0 + hyper))
    span1 = jnp.exp(-steps * mode_rate)
    span2 = span1 * span1
    span4 = span2 * span2
    block_decay = span4 * span4
    overlap = jnp.sum(gain * grow, axis=0, keepdims=True)

    for tile in range(tiles):
        ln = pl.ds(tile * LANES, LANES)
        xf[0, tile, :rows, :] = xb[0, tile].astype(jnp.float32)
        w0, w1, w2 = tap_rows(0, tile)
        prev1, prev2 = previous(0, tile, steps - 1), previous(0, tile, steps - 2)
        for k in range(steps):
            now = xf[0, tile, pl.ds(k, SUBS, stride=steps), :]
            sb[tile, k] = w0 * now + w1 * prev1 + w2 * prev2
            prev1, prev2 = now, prev1

        time = lax.broadcasted_iota(jnp.int32, (steps, LANES), 0).astype(jnp.float32)
        response = add_up([
            spread(gain, r, tile, steps) * jnp.exp(-spread(mode_rate, r, tile, steps) * time)
            for r in range(order)
        ])
        impulse[tile] = response
        impulse[tile, 0:1, :] = response[0:1, :] + skip[0:1, ln]
        for r in range(order):
            far[tile, r] = spread(gain, r, tile) * jnp.exp(-spread(mode_rate, r, tile) * distance)

    def gated_head(tile, mine, earlier):
        one, two = tap_rows(1, tile), tap_rows(2, tile)
        weight = [jnp.where(sub < 4, one[l], two[l]) for l in range(3)]
        joined = jnp.where(sub % 4 >= 2, mine, earlier)
        s = (
            weight[0] * joined
            + weight[1] * pltpu.roll(joined, 1, 0)
            + weight[2] * pltpu.roll(joined, 2, 0)
        )
        u = s * pltpu.roll(s, 4, 0)
        return u[2:3], u[3:4]

    def edge_rows(d, tile):
        if d == 0:
            return edges[8 * tile : 8 * tile + 8, :]
        if d not in reach:
            return jnp.zeros((8, LANES), jnp.float32)
        return inbox[d - 1, edge_from:, :].astype(jnp.float32)[8 * tile : 8 * tile + 8]

    def cut(table, tile):
        return table[:, tile * LANES : (tile + 1) * LANES]

    def enter(tile, carried, u0, u1):
        grown = cut(grow, tile)
        return carried + grown * (u0 + grown * u1)

    def after(tile, d, carried):
        u0, u1 = gated_head(tile, edge_rows(d, tile), edge_rows(d + 1, tile))
        end = states[tile] if d == 0 else inbox[d - 1, tile * order : (tile + 1) * order]
        return cut(block_decay, tile) * enter(tile, carried, u0, u1) + end.astype(jnp.float32)

    @pl.when(me == 1)
    def _():
        packets[1].wait_recv()
        for tile in range(tiles):
            both = after(tile, 0, after(tile, 1, jnp.zeros((order, LANES), jnp.float32)))
            outbox[tile * order : (tile + 1) * order] = both.astype(outbox.dtype)
        row = lax.broadcasted_iota(jnp.int32, (8 * tiles, LANES), 0)
        outbox[edge_from:] = jnp.where(row % 4 >= 2, 0.0, edges[...]).astype(outbox.dtype)
        greet_and_send()
        tail_packet.start()

    for tile in range(tiles):
        for first in range(0, steps, SUBS):
            total = [None] * SUBS
            for lag in range(0, first + 1, SUBS):
                source = first - lag
                u = [ub[tile, source + i] for i in range(SUBS)]
                for delay in range(max(0, lag - SUBS + 1), lag + SUBS):
                    tap = jnp.broadcast_to(impulse[tile, delay : delay + 1, :], (SUBS, LANES))
                    for i in range(SUBS):
                        k = source + i + delay - first
                        if 0 <= k < SUBS:
                            term = tap * u[i]
                            total[k] = term if total[k] is None else total[k] + term
            for k in range(SUBS):
                yb[tile, first + k] = total[k]
        for r in range(order):
            g = spread(gain, r, tile)
            total = ends[tile, r]
            for shift, table in ((1, span1), (2, span2), (4, span4)):
                total = total + jnp.where(
                    sub >= shift, spread(table, r, tile) * pltpu.roll(total, shift, 0), 0.0
                )
            ends[tile, r] = g * jnp.where(sub >= 1, pltpu.roll(total, 1, 0), 0.0)

    @pl.when(me > 0)
    def _():
        tail_packet.wait_recv()

    tails = tail_in[...].astype(jnp.float32)
    for tile in range(tiles):
        ln = pl.ds(tile * LANES, LANES)
        w1, w2 = taps[0, 1:2, ln], taps[0, 2:3, ln]
        t2, t1 = tails[2 * tile : 2 * tile + 1], tails[2 * tile + 1 : 2 * tile + 2]
        sb[tile, 0, 0:1, :] = sb[tile, 0, 0:1, :] + w1 * t1 + w2 * t2
        sb[tile, 1, 0:1, :] = sb[tile, 1, 0:1, :] + w2 * t1

    carried = [jnp.zeros((order, LANES), jnp.float32)] * tiles
    for d in reversed(reach):
        @pl.when(hears(d) & (me != 1))
        def _():
            packets[d].wait_recv()

        carried = [after(tile, d, carried[tile]) for tile in range(tiles)]

    for tile in range(tiles):
        ln = pl.ds(tile * LANES, LANES)
        u0, u1 = gated_head(tile, edge_rows(0, tile), edge_rows(1, tile))
        entry = enter(tile, carried[tile], u0, u1)
        direct = skip[0:1, ln]
        yb[tile, 0, 0:1, :] = yb[tile, 0, 0:1, :] + direct * u0 - cut(overlap, tile) * u1
        yb[tile, 1, 0:1, :] = yb[tile, 1, 0:1, :] + direct * u1

        a = [spread(decay, r, tile) for r in range(order)]
        modes = [
            ends[tile, r] + far[tile, r] * jnp.broadcast_to(entry[r : r + 1, :], (SUBS, LANES))
            for r in range(order)
        ]

        def finish(k, e):
            e = [a[r] * e[r] for r in range(order)]
            of[tile, pl.ds(k, SUBS, stride=steps), :] = sb[tile, k] * (yb[tile, k] + add_up(e))
            return e

        lax.fori_loop(0, steps, finish, modes, unroll=8)
        ob[:, ln] = of[tile, :rows, :].astype(ob.dtype)

    for d in reach:
        @pl.when(speaks(d))
        def _():
            packets[d].wait_send()

    @pl.when(me < count - 1)
    def _():
        tail_packet.wait_send()


def deliver(ob, out_hbm, sems):
    height = ob.shape[0] // CHUNKS
    stores = [
        pltpu.make_async_copy(
            ob.at[pl.ds(i * height, height), :], out_hbm.at[pl.ds(i * height, height), :], sems.at[i]
        )
        for i in range(CHUNKS)
    ]
    for store in stores:
        store.start()
    for store in stores:
        store.wait()


def body(hyena_in, short_taps, filter_residue, filter_rate, hyena_skip):
    count = lax.axis_size("ctx")
    _, rows, channels = hyena_in.shape
    order = filter_rate.shape[1]
    steps, tiles = rows // SUBS, channels // LANES
    f32, bf16 = jnp.float32, jnp.bfloat16
    signal = pltpu.VMEM((tiles, steps, SUBS, LANES), f32)
    vmem = pl.BlockSpec(memory_space=pltpu.VMEM)
    packet = (order + 8) * tiles
    per_mode = pltpu.VMEM((tiles, order, SUBS, LANES), f32)
    result = pl.pallas_call(
        functools.partial(exchange, count),
        out_shape=jax.ShapeDtypeStruct((rows, channels), bf16),
        in_specs=[pl.BlockSpec(memory_space=pltpu.HBM)] * 5,
        out_specs=vmem,
        scratch_shapes=[
            signal,
            signal,
            pltpu.VMEM((tiles, rows + steps, LANES), f32),
            pltpu.VMEM((3, tiles, rows, LANES), bf16),
            pltpu.VMEM((3, tiles, rows + steps, LANES), f32),
            pltpu.VMEM((3, 3, channels), f32),
            pltpu.VMEM((order, channels), f32),
            pltpu.VMEM((order, channels), f32),
            pltpu.VMEM((1, channels), f32),
            signal,
            pltpu.VMEM((8 * tiles, LANES), f32),
            pltpu.VMEM((tiles, order, LANES), f32),
            pltpu.VMEM((16, LANES), f32),
            pltpu.VMEM((packet, LANES), bf16),
            pltpu.VMEM((16, LANES), bf16),
            pltpu.VMEM((count - 2, packet, LANES), bf16),
            pltpu.VMEM((16, LANES), bf16),
            per_mode,
            per_mode,
            per_mode,
            pltpu.VMEM((tiles, steps, LANES), f32),
            pltpu.SemaphoreType.DMA((4,)),
            pltpu.SemaphoreType.DMA((3, tiles)),
            pltpu.SemaphoreType.DMA((count - 2,)),
            pltpu.SemaphoreType.DMA((count - 2,)),
            pltpu.SemaphoreType.DMA((2,)),
        ],
        compiler_params=pltpu.CompilerParams(
            collective_id=0, has_side_effects=True, vmem_limit_bytes=8 << 20
        ),
    )(*(
        pltpu.with_memory_space_constraint(value, pltpu.HBM)
        for value in (
            hyena_in, short_taps, filter_residue.T, filter_rate.T, hyena_skip.reshape(1, channels)
        )
    ))
    return pl.pallas_call(
        deliver,
        out_shape=jax.ShapeDtypeStruct((rows, channels), bf16),
        in_specs=[vmem],
        out_specs=pl.BlockSpec(memory_space=pltpu.HBM),
        scratch_shapes=[pltpu.SemaphoreType.DMA((CHUNKS,))],
        compiler_params=pltpu.CompilerParams(vmem_limit_bytes=1 << 20),
    )(result)


def solution(mesh):
    return jax.shard_map(
        body,
        mesh=mesh,
        in_specs=(P(None, "ctx", "mp"), P(None, None, "mp"), P("mp", None), P("mp", None), P("mp")),
        out_specs=P("ctx", "mp"),
        check_vma=False,
    )
```

```python
import functools

import jax
import jax.numpy as jnp
from jax import lax
from jax.experimental import pallas as pl
from jax.experimental.pallas import tpu as pltpu
from jax.sharding import PartitionSpec as P

MESH = pl.DeviceIdType.MESH
SUBS = 8
LANES = 128
CHUNKS = 4


def add_up(terms):
    while len(terms) > 1:
        pairs = [terms[i] + terms[i + 1] for i in range(0, len(terms) - 1, 2)]
        terms = pairs + terms[2 * len(pairs) :]
    return terms[0]


def exchange(
    count, x_hbm, taps_hbm, res_hbm, rate_hbm, skip_hbm, ob,
    yb, sb, of, xb, xf, taps, res, rate, skip, ub, edges, states, gate_tail,
    outbox, tail_out, inbox, tail_in, ends, near, far, impulse,
    load_sems, x_sems, send_sems, recv_sems, tail_sems,
):
    me = lax.axis_index("ctx")
    tiles, rows = xb.shape[1:3]
    order = rate.shape[0]
    steps = rows // SUBS
    edge_from = tiles * order
    reach = range(1, count - 1)

    def hears(d):
        return (me > d) | (me == 1) if d == 1 else me > d

    loads = [
        pltpu.make_async_copy(source, target, load_sems.at[i])
        for i, (source, target) in enumerate(
            [(rate_hbm, rate), (res_hbm, res), (taps_hbm, taps), (skip_hbm, skip)]
        )
    ]
    streams = [
        [
            pltpu.make_async_copy(
                x_hbm.at[p, :, pl.ds(tile * LANES, LANES)], xb.at[p, tile], x_sems.at[p, tile]
            )
            for p in range(3)
        ]
        for tile in range(tiles)
    ]
    loads[0].start()
    for p in (1, 2, 0):
        for tile in range(tiles):
            streams[tile][p].start()
    barrier = pltpu.get_barrier_semaphore()
    for d in range(1, count):
        @pl.when((me > d) | ((me == d) & (d == 1)))
        def _():
            pl.semaphore_signal(
                barrier, inc=1, device_id={"ctx": lax.rem(me - d + count, count)},
                device_id_type=MESH,
            )

    for load in loads[1:]:
        load.start()

    for d in reach:
        @pl.when(jnp.logical_not(hears(d)))
        def _():
            inbox[d - 1] = jnp.zeros(inbox.shape[1:], inbox.dtype)

    @pl.when(me == 0)
    def _():
        tail_in[...] = jnp.zeros_like(tail_in)

    gate_tail[...] = jnp.zeros_like(gate_tail)
    sub = lax.broadcasted_iota(jnp.int32, (SUBS, LANES), 0)
    distance = (sub * steps).astype(jnp.float32)
    remaining = ((SUBS - 1 - sub) * steps).astype(jnp.float32)

    def spread(table, r, tile, height=SUBS):
        return jnp.broadcast_to(
            table[r : r + 1, tile * LANES : (tile + 1) * LANES], (height, LANES)
        )

    loads[0].wait()
    mode_rate = rate[...]
    decay = jnp.exp(-mode_rate)
    for tile in range(tiles):
        for r in range(order):
            near[tile, r] = jnp.exp(-spread(mode_rate, r, tile) * remaining)
    for load in loads[1:]:
        load.wait()

    def send(out, box, d, send_sem, recv_sem):
        return pltpu.make_async_remote_copy(
            src_ref=out, dst_ref=box, send_sem=send_sem, recv_sem=recv_sem,
            device_id={"ctx": lax.rem(me + d, count)}, device_id_type=MESH,
        )

    packets = {
        d: send(outbox, inbox.at[d - 1], d, send_sems.at[d - 1], recv_sems.at[d - 1]) for d in reach
    }
    tail_packet = send(tail_out, tail_in, 1, tail_sems.at[0], tail_sems.at[1])

    def speaks(d):
        return me + d < count if d == 1 else (me > 0) & (me + d < count)

    def greet_and_send():
        expected = jnp.where(me == 0, 1, count - 1 - me)

        @pl.when(me < count - 1)
        def _():
            pl.semaphore_wait(barrier, expected)

        for d in reach:
            @pl.when(speaks(d))
            def _():
                packets[d].start()

    def previous(p, tile, k):
        last = xf[p, tile, pl.ds(k, SUBS, stride=steps), :]
        return jnp.where(sub == 0, 0.0, pltpu.roll(last, 1, 0))

    def tap_rows(p, tile):
        ln = pl.ds(tile * LANES, LANES)
        return [jnp.broadcast_to(taps[p, l : l + 1, ln], (SUBS, LANES)) for l in range(3)]

    for tile in range(tiles):
        for p in (1, 2):
            streams[tile][p].wait()
            first = tile * 8 + (p - 1) * 4
            edges[first : first + 2, :] = xb[p, tile, rows - 16 : rows, :].astype(jnp.float32)[14:16]
            edges[first + 2 : first + 4, :] = xb[p, tile, 0:16, :].astype(jnp.float32)[0:2]

    for tile in range(tiles):
        for p in (1, 2):
            xf[p, tile, :rows, :] = xb[p, tile].astype(jnp.float32)
        weight = {p: tap_rows(p, tile) for p in (1, 2)}
        a = [spread(decay, r, tile) for r in range(order)]

        def gate(k, carry, opening=False):
            prev1, prev2, h = carry
            now = [xf[p, tile, pl.ds(k, SUBS, stride=steps), :] for p in (1, 2)]
            s = [
                weight[p][0] * now[p - 1] + weight[p][1] * prev1[p - 1] + weight[p][2] * prev2[p - 1]
                for p in (1, 2)
            ]
            u = s[0] * s[1]
            if opening:
                u = jnp.where(sub == 0, 0.0, u)
            ub[tile, k] = u
            return now, prev1, [a[r] * h[r] + u for r in range(order)]

        start = (
            [previous(p, tile, steps - 1) for p in (1, 2)],
            [previous(p, tile, steps - 2) for p in (1, 2)],
            [jnp.zeros((SUBS, LANES), jnp.float32)] * order,
        )
        start = gate(1, gate(0, start, True), True)
        _, _, h = lax.fori_loop(2, steps, gate, start, unroll=6)
        for r in range(order):
            ends[tile, r] = h[r]
            states[tile, r : r + 1, :] = jnp.sum(near[tile, r] * h[r], axis=0, keepdims=True)

    for tile in range(tiles):
        outbox[tile * order : (tile + 1) * order] = states[tile].astype(outbox.dtype)
    outbox[edge_from:] = edges[...].astype(outbox.dtype)

    @pl.when(me != 1)
    def _():
        greet_and_send()

    for tile in range(tiles):
        streams[tile][0].wait()
        last = xb[0, tile, rows - 16 : rows, :].astype(jnp.float32)
        gate_tail[2 * tile : 2 * tile + 2, :] = last[14:16]
    tail_out[...] = gate_tail[...].astype(tail_out.dtype)

    @pl.when((me < count - 1) & (me != 1))
    def _():
        tail_packet.start()

    grow = jnp.exp(mode_rate)
    hyper = jnp.tanh(mode_rate)
    gain = res[...] * jnp.sqrt(2.0 * hyper / (1.0 + hyper))
    span1 = jnp.exp(-steps * mode_rate)
    span2 = span1 * span1
    span4 = span2 * span2
    block_decay = span4 * span4
    overlap = jnp.sum(gain * grow, axis=0, keepdims=True)

    for tile in range(tiles):
        ln = pl.ds(tile * LANES, LANES)
        xf[0, tile, :rows, :] = xb[0, tile].astype(jnp.float32)
        w0, w1, w2 = tap_rows(0, tile)
        prev1, prev2 = previous(0, tile, steps - 1), previous(0, tile, steps - 2)
        for k in range(steps):
            now = xf[0, tile, pl.ds(k, SUBS, stride=steps), :]
            sb[tile, k] = w0 * now + w1 * prev1 + w2 * prev2
            prev1, prev2 = now, prev1

        time = lax.broadcasted_iota(jnp.int32, (steps, LANES), 0).astype(jnp.float32)
        response = add_up([
            spread(gain, r, tile, steps) * jnp.exp(-spread(mode_rate, r, tile, steps) * time)
            for r in range(order)
        ])
        impulse[tile] = response
        impulse[tile, 0:1, :] = response[0:1, :] + skip[0:1, ln]
        for r in range(order):
            far[tile, r] = spread(gain, r, tile) * jnp.exp(-spread(mode_rate, r, tile) * distance)

    def gated_head(tile, mine, earlier):
        one, two = tap_rows(1, tile), tap_rows(2, tile)
        weight = [jnp.where(sub < 4, one[l], two[l]) for l in range(3)]
        joined = jnp.where(sub % 4 >= 2, mine, earlier)
        s = (
            weight[0] * joined
            + weight[1] * pltpu.roll(joined, 1, 0)
            + weight[2] * pltpu.roll(joined, 2, 0)
        )
        u = s * pltpu.roll(s, 4, 0)
        return u[2:3], u[3:4]

    def edge_rows(d, tile):
        if d == 0:
            return edges[8 * tile : 8 * tile + 8, :]
        if d not in reach:
            return jnp.zeros((8, LANES), jnp.float32)
        return inbox[d - 1, edge_from:, :].astype(jnp.float32)[8 * tile : 8 * tile + 8]

    def cut(table, tile):
        return table[:, tile * LANES : (tile + 1) * LANES]

    def enter(tile, carried, u0, u1):
        grown = cut(grow, tile)
        return carried + grown * (u0 + grown * u1)

    def after(tile, d, carried):
        u0, u1 = gated_head(tile, edge_rows(d, tile), edge_rows(d + 1, tile))
        end = states[tile] if d == 0 else inbox[d - 1, tile * order : (tile + 1) * order]
        return cut(block_decay, tile) * enter(tile, carried, u0, u1) + end.astype(jnp.float32)

    @pl.when(me == 1)
    def _():
        packets[1].wait_recv()
        for tile in range(tiles):
            both = after(tile, 0, after(tile, 1, jnp.zeros((order, LANES), jnp.float32)))
            outbox[tile * order : (tile + 1) * order] = both.astype(outbox.dtype)
        row = lax.broadcasted_iota(jnp.int32, (8 * tiles, LANES), 0)
        outbox[edge_from:] = jnp.where(row % 4 >= 2, 0.0, edges[...]).astype(outbox.dtype)
        greet_and_send()
        tail_packet.start()

    for tile in range(tiles):
        for first in range(0, steps, SUBS):
            total = [None] * SUBS
            for lag in range(0, first + 1, SUBS):
                source = first - lag
                u = [ub[tile, source + i] for i in range(SUBS)]
                for delay in range(max(0, lag - SUBS + 1), lag + SUBS):
                    tap = jnp.broadcast_to(impulse[tile, delay : delay + 1, :], (SUBS, LANES))
                    for i in range(SUBS):
                        k = source + i + delay - first
                        if 0 <= k < SUBS:
                            term = tap * u[i]
                            total[k] = term if total[k] is None else total[k] + term
            for k in range(SUBS):
                yb[tile, first + k] = total[k]
        for r in range(order):
            g = spread(gain, r, tile)
            total = ends[tile, r]
            for shift, table in ((1, span1), (2, span2), (4, span4)):
                total = total + jnp.where(
                    sub >= shift, spread(table, r, tile) * pltpu.roll(total, shift, 0), 0.0
                )
            ends[tile, r] = g * jnp.where(sub >= 1, pltpu.roll(total, 1, 0), 0.0)

    @pl.when(me > 0)
    def _():
        tail_packet.wait_recv()

    tails = tail_in[...].astype(jnp.float32)
    for tile in range(tiles):
        ln = pl.ds(tile * LANES, LANES)
        w1, w2 = taps[0, 1:2, ln], taps[0, 2:3, ln]
        t2, t1 = tails[2 * tile : 2 * tile + 1], tails[2 * tile + 1 : 2 * tile + 2]
        sb[tile, 0, 0:1, :] = sb[tile, 0, 0:1, :] + w1 * t1 + w2 * t2
        sb[tile, 1, 0:1, :] = sb[tile, 1, 0:1, :] + w2 * t1

    carried = [jnp.zeros((order, LANES), jnp.float32)] * tiles
    for d in reversed(reach):
        @pl.when(hears(d) & (me != 1))
        def _():
            packets[d].wait_recv()

        carried = [after(tile, d, carried[tile]) for tile in range(tiles)]

    for tile in range(tiles):
        ln = pl.ds(tile * LANES, LANES)
        u0, u1 = gated_head(tile, edge_rows(0, tile), edge_rows(1, tile))
        entry = enter(tile, carried[tile], u0, u1)
        direct = skip[0:1, ln]
        yb[tile, 0, 0:1, :] = yb[tile, 0, 0:1, :] + direct * u0 - cut(overlap, tile) * u1
        yb[tile, 1, 0:1, :] = yb[tile, 1, 0:1, :] + direct * u1

        a = [spread(decay, r, tile) for r in range(order)]
        modes = [
            ends[tile, r] + far[tile, r] * jnp.broadcast_to(entry[r : r + 1, :], (SUBS, LANES))
            for r in range(order)
        ]

        def finish(k, e):
            e = [a[r] * e[r] for r in range(order)]
            of[tile, pl.ds(k, SUBS, stride=steps), :] = sb[tile, k] * (yb[tile, k] + add_up(e))
            return e

        lax.fori_loop(0, steps, finish, modes, unroll=8)
        ob[:, ln] = of[tile, :rows, :].astype(ob.dtype)

    for d in reach:
        @pl.when(speaks(d))
        def _():
            packets[d].wait_send()

    @pl.when(me < count - 1)
    def _():
        tail_packet.wait_send()


def deliver(ob, out_hbm, sems):
    height = ob.shape[0] // CHUNKS
    stores = [
        pltpu.make_async_copy(
            ob.at[pl.ds(i * height, height), :], out_hbm.at[pl.ds(i * height, height), :], sems.at[i]
        )
        for i in range(CHUNKS)
    ]
    for store in stores:
        store.start()
    for store in stores:
        store.wait()


def body(hyena_in, short_taps, filter_residue, filter_rate, hyena_skip):
    count = lax.axis_size("ctx")
    _, rows, channels = hyena_in.shape
    order = filter_rate.shape[1]
    steps, tiles = rows // SUBS, channels // LANES
    f32, bf16 = jnp.float32, jnp.bfloat16
    signal = pltpu.VMEM((tiles, steps, SUBS, LANES), f32)
    vmem = pl.BlockSpec(memory_space=pltpu.VMEM)
    packet = (order + 8) * tiles
    per_mode = pltpu.VMEM((tiles, order, SUBS, LANES), f32)
    result = pl.pallas_call(
        functools.partial(exchange, count),
        out_shape=jax.ShapeDtypeStruct((rows, channels), bf16),
        in_specs=[pl.BlockSpec(memory_space=pltpu.HBM)] * 5,
        out_specs=vmem,
        scratch_shapes=[
            signal,
            signal,
            pltpu.VMEM((tiles, rows + steps, LANES), f32),
            pltpu.VMEM((3, tiles, rows, LANES), bf16),
            pltpu.VMEM((3, tiles, rows + steps, LANES), f32),
            pltpu.VMEM((3, 3, channels), f32),
            pltpu.VMEM((order, channels), f32),
            pltpu.VMEM((order, channels), f32),
            pltpu.VMEM((1, channels), f32),
            signal,
            pltpu.VMEM((8 * tiles, LANES), f32),
            pltpu.VMEM((tiles, order, LANES), f32),
            pltpu.VMEM((16, LANES), f32),
            pltpu.VMEM((packet, LANES), bf16),
            pltpu.VMEM((16, LANES), bf16),
            pltpu.VMEM((count - 2, packet, LANES), bf16),
            pltpu.VMEM((16, LANES), bf16),
            per_mode,
            per_mode,
            per_mode,
            pltpu.VMEM((tiles, steps, LANES), f32),
            pltpu.SemaphoreType.DMA((4,)),
            pltpu.SemaphoreType.DMA((3, tiles)),
            pltpu.SemaphoreType.DMA((count - 2,)),
            pltpu.SemaphoreType.DMA((count - 2,)),
            pltpu.SemaphoreType.DMA((2,)),
        ],
        compiler_params=pltpu.CompilerParams(
            collective_id=0, has_side_effects=True, vmem_limit_bytes=8 << 20
        ),
    )(*(
        pltpu.with_memory_space_constraint(value, pltpu.HBM)
        for value in (
            hyena_in, short_taps, filter_residue.T, filter_rate.T, hyena_skip.reshape(1, channels)
        )
    ))
    return pl.pallas_call(
        deliver,
        out_shape=jax.ShapeDtypeStruct((rows, channels), bf16),
        in_specs=[vmem],
        out_specs=pl.BlockSpec(memory_space=pltpu.HBM),
        scratch_shapes=[pltpu.SemaphoreType.DMA((CHUNKS,))],
        compiler_params=pltpu.CompilerParams(vmem_limit_bytes=1 << 20),
    )(result)


def solution(mesh):
    return jax.shard_map(
        body,
        mesh=mesh,
        in_specs=(P(None, "ctx", "mp"), P(None, None, "mp"), P("mp", None), P("mp", None), P("mp")),
        out_specs=P("ctx", "mp"),
        check_vma=False,
    )
```
